256 devices in a mesh: gx: 8 (over x, core), gy: 32 (over z, y).
Axes of the slice: x: 4, y: 4, z: 8, core: 2. Of those that a mesh axis runs over, the one named last changes fastest.
Arguments:
- old_basis: float32 [64, 256, 16384], P(None, 'gx', 'gy'), may hold values from -6 to 6
- new_block: float32 [32, 256, 16384], P(None, 'gx', 'gy'), may hold values from -640 to 640
- source_matrix: float32 [32, 256, 16384], P(None, 'gx', 'gy'), may hold values from -82 to 82
- region_map: int32 [256, 16384], P('gx', 'gy'), may hold values from 0 to 7
- conductivity: float32 [8], replicated, may hold values from 0.1 to 1
- damping: float32 [8], replicated, may hold values from 0.2 to 2
- drift_speed: float32 [8], replicated, may hold values from 0.2 to 2
- heat_capacity: float32 [8], replicated, may hold values from 0.5 to 2
- sensor_cells: int32 [16], replicated, may hold values from 0 to 4194303
Outputs:
- new_basis: float32 [32, 256, 16384], P(None, 'gx', 'gy')
- applied_block: float32 [32, 256, 16384], P(None, 'gx', 'gy')
- stiff_block: float32 [96, 32], replicated
- stiff_row: float32 [32, 64], replicated
- capacity_block: float32 [96, 32], replicated
- sensor_block: float32 [16, 32], replicated
- source_block: float32 [32, 32], replicated
The draws below stay inside these ranges and needn't reach their ends.
All inputs are finite; a program needn't handle non-finite values.
Results may differ from the reference program's by a relative error of at most 0.0003.
Values sent between devices are 32-bit elements; how exact they have to be, the bound alone decides.
No kernel may reach another device: no remote copies, remote signals or barrier semaphores. Data moves between devices by JAX's collectives and lax.ppermute only.
A program may use at most 128 MiB of HBM per device.

```python
import math
import jax
import jax.numpy as jnp
from jax import lax

K = 64
M = 32
MB = 32
NREG = 8
P_SIZE = 16
NZ = 64
NX = 256
NY = 256


def shared_fields(key):
    region = jax.random.randint(jax.random.fold_in(key, 11), (NX, NY * NZ), 0, NREG)
    capacity = jnp.exp(jax.random.uniform(jax.random.fold_in(key, 12), (NREG,), jnp.float32, math.log(0.5), math.log(2.0)))
    capacity = jnp.clip(capacity, 0.5, 2.0)
    own_fields = jax.random.normal(jax.random.fold_in(key, 13), (K, NX, NY * NZ), jnp.float32)
    common_field = jnp.clip(jax.random.normal(jax.random.fold_in(key, 15), (NX, NY * NZ), jnp.float32), -6.0, 6.0)
    tilt = jax.random.uniform(jax.random.fold_in(key, 16), (K,), jnp.float32, -1.0, 1.0)
    basis_fields = jnp.clip(own_fields + 0.05 * tilt[:, None, None] * common_field[None], -6.0, 6.0)
    rough_part = jnp.clip(jax.random.normal(jax.random.fold_in(key, 14), (M, NX, NY * NZ), jnp.float32), -6.0, 6.0)
    along_x = jnp.arange(NX).astype(jnp.float32) / NX
    along_y = (jnp.arange(NY * NZ) // NZ).astype(jnp.float32) / NY
    amplitude = jnp.exp(math.log(3.0) * along_x)[:, None] * jnp.exp(math.log(3.0) * along_y)[None, :]
    return (region, capacity, basis_fields, rough_part, amplitude)


def draw_region_map(key, part):
    region, capacity, basis_fields, rough_part, amplitude = shared_fields(key)
    return region


def draw_heat_capacity(key, part):
    region, capacity, basis_fields, rough_part, amplitude = shared_fields(key)
    return capacity


def draw_old_basis(key, part):
    region, capacity, basis_fields, rough_part, amplitude = shared_fields(key)
    return basis_fields


def draw_new_block(key, part):
    region, capacity, basis_fields, rough_part, amplitude = shared_fields(key)
    key = jax.random.fold_in(key, 4)
    scale_key, first_key, second_key = jax.random.split(key, 3)
    column_scale = jnp.exp(jax.random.uniform(scale_key, (M,), jnp.float32, math.log(0.1), math.log(10.0)))
    first_coef = jax.random.uniform(first_key, (M,), jnp.float32, 2.0, 5.0)
    second_coef = jax.random.uniform(second_key, (M,), jnp.float32, 2.0, 5.0)
    residue = rough_part
    mixed = first_coef[:, None, None] * basis_fields[:M] + second_coef[:, None, None] * basis_fields[M:2 * M] + 0.05 * amplitude[None] * residue
    return column_scale[:, None, None] * mixed


def draw_source_matrix(key, part):
    region, capacity, basis_fields, rough_part, amplitude = shared_fields(key)
    key = jax.random.fold_in(key, 5)
    own_part = jnp.clip(jax.random.normal(key, (MB, NX, NY * NZ), jnp.float32), -6.0, 6.0)
    mixed = amplitude[None] * (rough_part[:MB] + 0.5 * own_part)
    return mixed


def with_ends(array, key, smallest, top_value):
    longest = array.shape.index(max(array.shape))
    spots = []
    for shift in (0, 1):
        where = [jax.random.randint(jax.random.fold_in(key, axis), (), 0, length) for axis, length in enumerate(array.shape)]
        where[longest] = (where[longest] + shift) % array.shape[longest]
        spots.append(tuple(where))
    return array.at[spots[0]].set(smallest).at[spots[1]].set(top_value)


def setup_inputs(seed: int = 0) -> dict:
    arg_keys = jax.random.split(jax.random.key(seed), 10)
    old_basis = draw_old_basis(jax.random.fold_in(arg_keys[9], 71), 0)
    new_block = draw_new_block(jax.random.fold_in(arg_keys[9], 71), 0)
    source_matrix = draw_source_matrix(jax.random.fold_in(arg_keys[9], 71), 0)
    region_map = draw_region_map(jax.random.fold_in(arg_keys[9], 71), 0)
    conductivity = jnp.clip(jnp.exp(jax.random.uniform(arg_keys[4], (NREG,), jnp.float32, math.log(0.1), math.log(1.0))), 0.1, 1.0)
    damping = jnp.clip(jnp.exp(jax.random.uniform(arg_keys[5], (NREG,), jnp.float32, math.log(0.2), math.log(2.0))), 0.2, 2.0)
    drift_speed = jnp.clip(jnp.exp(jax.random.uniform(arg_keys[6], (NREG,), jnp.float32, math.log(0.2), math.log(2.0))), 0.2, 2.0)
    heat_capacity = draw_heat_capacity(jax.random.fold_in(arg_keys[9], 71), 0)
    sensor_cells = with_ends(jax.random.randint(arg_keys[8], (P_SIZE,), 0, NX * NY * NZ), jax.random.fold_in(arg_keys[8], 1), 0, (NX * NY * NZ) - 1).astype(jnp.int32)
    return dict(old_basis=old_basis, new_block=new_block, source_matrix=source_matrix, region_map=region_map, conductivity=conductivity, damping=damping, drift_speed=drift_speed, heat_capacity=heat_capacity, sensor_cells=sensor_cells)


PRECISE = lax.Precision.HIGHEST

def diffusion(vectors, near_vectors, near_conduct, conduct):
    summed = jnp.zeros_like(vectors)
    for near_vector, near_coef in zip(near_vectors, near_conduct):
        summed = summed + 0.5 * (conduct + near_coef) * (near_vector - vectors)
    return summed

def beside_all(padded_array):
    return [padded_array[:-2, 1:-1, 1:-1], padded_array[2:, 1:-1, 1:-1], padded_array[1:-1, :-2, 1:-1], padded_array[1:-1, 2:, 1:-1], padded_array[1:-1, 1:-1, :-2], padded_array[1:-1, 1:-1, 2:]]

def grid_operator(vectors, conduct, drift_cell, loss_cell, transposed):
    near_vectors = beside_all(jnp.pad(vectors, 1))
    result = diffusion(vectors, near_vectors, beside_all(jnp.pad(conduct, 1)), conduct) - loss_cell * vectors
    if transposed:
        return result - drift_cell * vectors + beside_all(jnp.pad(drift_cell, 1))[1] * near_vectors[1]
    return result - drift_cell * (vectors - near_vectors[0])

def contract(left_side, right_side):
    return jnp.einsum('acd,bcd->ab', left_side, right_side, precision=PRECISE)

def lower_inverse(gram_matrix):
    factor = jnp.linalg.cholesky(gram_matrix)
    identity = jnp.eye(gram_matrix.shape[0], dtype=gram_matrix.dtype)
    return jax.scipy.linalg.solve_triangular(factor, identity, lower=True)

def reference(old_basis, new_block, source_matrix, region_map, conductivity, damping, drift_speed, heat_capacity, sensor_cells):
    volume = 1.0 / (NX * NY * NZ)
    grid_shape = (NX, NY, NZ)
    conduct = conductivity[region_map].reshape(grid_shape)
    drift_cell = drift_speed[region_map].reshape(grid_shape)
    loss_cell = (damping * heat_capacity)[region_map].reshape(grid_shape)
    capacity_cell = heat_capacity[region_map]

    def forward(vectors):
        return grid_operator(vectors.reshape(grid_shape), conduct, drift_cell, loss_cell, False).reshape(NX, NY * NZ)

    def project(target):
        weights = contract(old_basis, target) * volume
        return target - jnp.einsum('ab,acd->bcd', weights, old_basis, precision=PRECISE)
    cleaned = project(project(new_block))
    gram_inverse = lower_inverse(contract(cleaned, cleaned) * volume)
    new_basis = jnp.einsum('ab,bcd->acd', gram_inverse, cleaned, precision=PRECISE)
    applied_block = lax.map(forward, new_basis)
    massed = capacity_cell * new_basis
    stiff_block = jnp.concatenate([contract(old_basis, applied_block), contract(new_basis, applied_block)], axis=0) * volume

    def row_entries(basis_vector):
        return jnp.einsum('cd,bcd->b', forward(basis_vector), new_basis, precision=PRECISE)
    stiff_row = lax.map(row_entries, old_basis).T * volume
    capacity_block = jnp.concatenate([contract(old_basis, massed), contract(new_basis, massed)], axis=0) * volume
    sensor_block = new_basis.reshape(M, NX * NY * NZ)[:, sensor_cells].T
    source_block = contract(new_basis, source_matrix) * volume
    return (new_basis, applied_block, stiff_block, stiff_row, capacity_block, sensor_block, source_block)
```

```python
import functools

import jax
import jax.numpy as jnp
from jax import lax
from jax.experimental import pallas as pl
from jax.experimental.pallas import tpu as pltpu
from jax.sharding import PartitionSpec as P

NZ = 64
LANES = 128
OLD = 64
NEW = 32
ALL = OLD + NEW
ROWS = 32
CHUNKS = 4
HALF = ROWS // 2
GROUP = 2
PARTS = 3
FACE = ALL + 8
XFACE = ALL + 16
F32 = jnp.float32
BF16 = jnp.bfloat16
HIGH = lax.Precision.HIGHEST
VMEM_LIMIT = 56 * 1024 * 1024


def split(value, count):
    pieces = []
    for _ in range(count):
        piece = value.astype(BF16)
        pieces.append(piece)
        value = value - piece.astype(F32)
    return pieces


def lanes_of(shape):
    return lax.broadcasted_iota(jnp.int32, shape, len(shape) - 1)


def rows_of(shape):
    return lax.broadcasted_iota(jnp.int32, shape, 0)


def field_row(refs, x):
    old_ref, new_ref = refs
    return jnp.concatenate(
        [old_ref[pl.ds(x, OLD, stride=ROWS), :], new_ref[pl.ds(x, NEW, stride=ROWS), :]], axis=0
    )


def lookup(region, table):
    result = jnp.zeros(region.shape, F32)
    for r in range(8):
        result = jnp.where(region == r, table[r], result)
    return result


def cell_fields(region_ref, conductivity, damping, drift_speed, heat_capacity):
    region = region_ref[...]
    conduct = jnp.zeros(region.shape, F32)
    drift = jnp.zeros(region.shape, F32)
    loss = jnp.zeros(region.shape, F32)
    capacity = jnp.zeros(region.shape, F32)
    for r in range(8):
        here = region == r
        conduct = jnp.where(here, conductivity[r], conduct)
        drift = jnp.where(here, drift_speed[r], drift)
        loss = jnp.where(here, damping[r] * heat_capacity[r], loss)
        capacity = jnp.where(here, heat_capacity[r], capacity)
    return conduct, drift, loss, capacity


def z_terms(conduct, z_index):
    low_z = jnp.where(z_index == 0, 0.0, pltpu.roll(conduct, 1, 1))
    high_z = jnp.where(z_index == NZ - 1, 0.0, pltpu.roll(conduct, conduct.shape[1] - 1, 1))
    return 0.5 * (conduct + low_z), 0.5 * (conduct + high_z)


def coef_writer(coef):
    def keep_coef(index, value):
        for j in range(CHUNKS):
            coef[index * CHUNKS + j] = value[:, j * LANES : (j + 1) * LANES]

    return keep_coef


def pack_kernel(
    region_ref, conductivity, damping, drift_speed, heat_capacity, shifts, edges, *refs
):
    old = refs[:CHUNKS]
    new = refs[CHUNKS : 2 * CHUNKS]
    y_top, y_low, x_top, x_low, coef = refs[2 * CHUNKS :]
    width = CHUNKS * LANES
    conduct, drift, loss, capacity = cell_fields(
        region_ref, conductivity, damping, drift_speed, heat_capacity
    )
    low_half = lanes_of((1, LANES)) < NZ
    first = (old[0], new[0])
    last = (old[CHUNKS - 1], new[CHUNKS - 1])

    def tail(rows, value):
        return jnp.broadcast_to(value, (rows, LANES))

    for r in range(HALF):
        near, far = field_row(last, r), field_row(last, r + HALF)
        y_top[r, 0:ALL, :] = jnp.where(low_half, pltpu.roll(near, NZ, 1), far)
        near, far = field_row(first, r), field_row(first, r + HALF)
        y_low[r, 0:ALL, :] = jnp.where(low_half, near, pltpu.roll(far, NZ, 1))
        near = conduct[r : r + 1, width - LANES :]
        far = conduct[r + HALF : r + HALF + 1, width - LANES :]
        y_top[r, ALL:FACE, :] = tail(8, jnp.where(low_half, pltpu.roll(near, NZ, 1), far))
        near = conduct[r : r + 1, :LANES]
        far = conduct[r + HALF : r + HALF + 1, :LANES]
        y_low[r, ALL:FACE, :] = tail(8, jnp.where(low_half, near, pltpu.roll(far, NZ, 1)))
    for j in range(CHUNKS):
        here = slice(j * LANES, (j + 1) * LANES)
        for out, row in ((x_top, ROWS - 1), (x_low, 0)):
            out[j, 0:ALL, :] = field_row((old[j], new[j]), row)
            out[j, ALL : ALL + 8, :] = tail(8, conduct[row : row + 1, here])
            out[j, ALL + 8 : XFACE, :] = tail(8, drift[row : row + 1, here])

    shape = (ROWS, width)
    lane = lanes_of(shape)
    row = rows_of(shape)
    z_index = lane % NZ
    z_down, z_up = z_terms(conduct, z_index)
    half = 0.5 * conduct
    from_low_y = 0.5 * (conduct + pltpu.roll(conduct, NZ, 1))
    from_high_y = 0.5 * (conduct + pltpu.roll(conduct, width - NZ, 1))
    from_low_x = 0.5 * (conduct + pltpu.roll(conduct, 1, 0))
    from_high_x = 0.5 * (conduct + pltpu.roll(conduct, ROWS - 1, 0))
    y_down = jnp.where(lane < NZ, 0.0, from_low_y)
    y_up = jnp.where(lane >= width - NZ, 0.0, from_high_y)
    x_down = jnp.where(row == 0, 0.0, from_low_x)
    x_up = jnp.where(row == ROWS - 1, 0.0, from_high_x)
    pull = jnp.where(row == 0, 0.0, drift)
    x_last = jnp.where(edges[0] == 1, 1.0, 0.0)
    y_last = jnp.where(edges[1] == 1, 1.0, 0.0)
    border = jnp.where(row == ROWS - 1, half * x_last, 0.0) + jnp.where(
        lane >= width - NZ, half * y_last, 0.0
    )
    keep_coef = coef_writer(coef)
    total = z_down + z_up + y_down + y_up + x_down + x_up + pull + loss + border
    keep_coef(0, x_down + pull)
    keep_coef(1, x_up)
    keep_coef(2, y_down)
    keep_coef(3, y_up)
    keep_coef(4, jnp.where(z_index == 0, 0.0, z_down))
    keep_coef(5, jnp.where(z_index == NZ - 1, 0.0, z_up))
    keep_coef(6, shifts[0] - total)
    keep_coef(7, capacity - shifts[1])


def gram_kernel(places, coef, *refs):
    old = refs[:CHUNKS]
    new = refs[CHUNKS : 2 * CHUNKS]
    source = refs[2 * CHUNKS : 3 * CHUNKS]
    out, sensed, first, second = refs[3 * CHUNKS :]
    low_half = lanes_of((1, LANES)) < NZ
    zero_rows = jnp.zeros((LANES - ALL, first.shape[1]), BF16)
    for stack in (first, second):
        stack[ALL:LANES, :] = zero_rows
        stack[LANES + ALL : 2 * LANES, :] = zero_rows

    def fill(stack, group):
        for r in range(GROUP):
            x = group * GROUP + r
            below = jnp.maximum(x - 1, 0)
            above = jnp.minimum(x + 1, ROWS - 1)
            mid = [field_row((old[j], new[j]), x) for j in range(CHUNKS)]
            swapped = [pltpu.roll(value, NZ, 1) for value in mid]
            for j in range(CHUNKS):
                here = pl.ds(j * LANES, LANES)
                refs_j = (old[j], new[j])
                left = jnp.where(low_half, swapped[max(j - 1, 0)], swapped[j])
                right = jnp.where(low_half, swapped[j], swapped[min(j + 1, CHUNKS - 1)])

                def scale(index):
                    return coef[index * CHUNKS + j, pl.ds(x, 1), :]

                value = mid[j]
                moved = (
                    scale(0) * field_row(refs_j, below)
                    + scale(1) * field_row(refs_j, above)
                    + scale(2) * left
                    + scale(3) * right
                    + scale(4) * pltpu.roll(value, 1, 1)
                    + scale(5) * pltpu.roll(value, LANES - 1, 1)
                    + scale(6) * value
                )
                at = pl.ds((r * CHUNKS + j) * LANES, LANES)
                high, low = split(value, 2)
                stack[0:ALL, at] = high
                stack[LANES : LANES + ALL, at] = low
                base = 2 * LANES
                for item in (moved, scale(7) * value):
                    high, low = split(item, 2)
                    stack[base : base + ALL, at] = high
                    stack[base + ALL : base + 2 * ALL, at] = low
                    base += 2 * ALL
                high, low = split(source[j][pl.ds(x, NEW, stride=ROWS), :], 2)
                stack[base : base + NEW, at] = high
                stack[base + NEW : base + 2 * NEW, at] = low

    def add(stack):
        out[...] += lax.dot_general(
            stack[...],
            stack[0 : 2 * LANES, :],
            (((1,), (1,)), ((), ())),
            preferred_element_type=F32,
        )

    out[...] = jnp.zeros(out.shape, F32)
    groups = ROWS // GROUP
    fill(first, 0)

    def step(i, carry):
        fill(second, 2 * i + 1)
        add(first)
        fill(first, jnp.minimum(2 * i + 2, groups - 1))
        add(second)
        return carry

    lax.fori_loop(0, groups // 2, step, 0)

    lane = lanes_of((ALL, LANES))

    def sense(p, total):
        place = places[p]
        inside = place >= 0
        place = jnp.maximum(place, 0)
        x = place // (CHUNKS * LANES)
        column = place % (CHUNKS * LANES)
        found = jnp.zeros((ALL, LANES), F32)
        for j in range(CHUNKS):
            hit = (lane == column - j * LANES) & inside
            found = jnp.where(hit, field_row((old[j], new[j]), x), found)
        return jnp.where(lane == p, jnp.sum(found, axis=1, keepdims=True), total)

    sensed[...] = lax.fori_loop(0, places.shape[0], sense, jnp.zeros((ALL, LANES), F32))


def fold(block, rows):
    return (
        block[0:rows, 0:LANES]
        + block[rows : 2 * rows, 0:LANES]
        + (block[0:rows, LANES:] + block[rows : 2 * rows, LANES:])
    )


def face_kernel(gram, sensed, y_own, y_near, x_own, x_near, out, diffs, scaled):
    tiles = HALF + CHUNKS
    zero_rows = jnp.zeros((LANES - ALL, tiles * LANES), BF16)
    scaled[ALL:LANES, :] = zero_rows
    scaled[LANES + ALL : 2 * LANES, :] = zero_rows
    for t in range(tiles):
        at = pl.ds(t * LANES, LANES)
        if t < HALF:
            own, near = y_own.at[t], y_near.at[t]
        else:
            own, near = x_own.at[t - HALF], x_near.at[t - HALF]
        value = own[0:ALL, :]
        diff = value - near[0:ALL, :]
        edge = 0.5 * (own[ALL : ALL + 1, :] + near[ALL : ALL + 1, :])
        weighted = edge * diff
        if t >= HALF:
            weighted = weighted + own[ALL + 8 : ALL + 9, :] * value
        high, low = split(diff, 2)
        diffs[0:ALL, at] = high
        diffs[ALL : 2 * ALL, at] = low
        high, low = split(weighted, 2)
        scaled[0:ALL, at] = high
        scaled[LANES : LANES + ALL, at] = low
    faces = lax.dot_general(
        diffs[...], scaled[...], (((1,), (1,)), ((), ())), preferred_element_type=F32
    )
    base = 2 * LANES
    overlap = (
        gram[0:ALL, 0:LANES]
        + gram[0:ALL, LANES:]
        + (gram[LANES : LANES + ALL, 0:LANES] + gram[LANES : LANES + ALL, LANES:])
    )
    moved = fold(gram[base : base + 2 * ALL, :], ALL) - fold(faces, ALL)
    base += 2 * ALL
    massed = fold(gram[base : base + 2 * ALL, :], ALL)
    base += 2 * ALL
    source = fold(gram[base : base + 2 * NEW, :], NEW)
    source = jnp.concatenate([source, jnp.zeros((LANES - NEW, LANES), F32)], axis=0).T
    source = pltpu.roll(source[0:ALL, :], ALL, 1)
    lane = lanes_of((ALL, LANES))
    row = rows_of((ALL, LANES))
    diagonal = jnp.sum(jnp.where(lane == row, massed, 0.0), axis=1, keepdims=True)
    upper = jnp.where(row >= lane, overlap, massed)
    out[0:ALL, :] = jnp.where(lane < ALL, upper, source)
    extra = jnp.where(lane == ALL + 16, diagonal, pltpu.roll(sensed[...], ALL, 1))
    out[ALL : 2 * ALL, :] = jnp.where(lane < ALL, moved, extra)


def small_dot(left, right):
    return lax.dot_general(
        left, right, (((1,), (0,)), ((), ())), preferred_element_type=F32, precision=HIGH
    )


def flip(block):
    rows, columns = block.shape
    if rows < LANES:
        block = jnp.concatenate([block, jnp.zeros((LANES - rows, columns), F32)], axis=0)
    if columns < LANES:
        block = jnp.concatenate([block, jnp.zeros((LANES, LANES - columns), F32)], axis=1)
    return block.T[0:columns, 0:rows]


def lower_inverse(gram):
    shape = (NEW, LANES)
    lane, row = lanes_of(shape), rows_of(shape)
    work = jnp.concatenate(
        [gram, jnp.zeros((NEW, LANES - NEW), F32)], axis=1
    ) + jnp.where(lane == row + NEW, 1.0, 0.0)
    for k in range(NEW):
        pivot = work[k : k + 1, k : k + 1]
        line = work[k : k + 1, :] / pivot
        factor = jnp.where(row[:, 0:1] > k, work[:, k : k + 1], 0.0)
        work = work - factor * line
    pivots = jnp.sum(jnp.where(lane == row, work, 0.0), axis=1, keepdims=True)
    return (work / jnp.sqrt(pivots))[:, NEW : 2 * NEW]


def basis_kernel(
    volume,
    region_ref,
    conductivity,
    damping,
    drift_speed,
    heat_capacity,
    shifts,
    summed,
    y_before,
    y_after,
    x_before,
    x_after,
    *refs,
):
    old = refs[:CHUNKS]
    new = refs[CHUNKS : 2 * CHUNKS]
    refs = refs[2 * CHUNKS :]
    basis_out, applied_out, stiff_block, stiff_row, capacity_block, sensor_block, source_block = refs[:7]
    coef, field, low_y, high_y, basis, applied, first, second, weights, sems = refs[7:]
    width = CHUNKS * LANES

    lane = lanes_of((ALL, LANES))
    row = rows_of((ALL, LANES))
    top = summed[0:ALL, :] * volume
    bottom = summed[ALL : 2 * ALL, :] * volume
    upper = jnp.where(lane < ALL, top, 0.0)
    low_part = jnp.where(lane <= row, upper, 0.0)
    high_part = jnp.where(lane > row, upper, 0.0)
    diagonal = jnp.where(lane == row, low_part, 0.0)
    overlap = (low_part - diagonal)[:, 0:ALL] + flip(low_part[:, 0:ALL])
    mass_diagonal = jnp.where(lane == row, bottom[:, ALL + 16 : ALL + 17], 0.0)
    massed = (high_part + mass_diagonal)[:, 0:ALL] + flip(high_part[:, 0:ALL])
    moved = flip(bottom[:, 0:ALL])
    source = top[:, ALL:LANES]
    sensed = summed[ALL : 2 * ALL, ALL : ALL + 16]

    old_gram = overlap[0:OLD, 0:OLD]
    first_weights = overlap[0:OLD, OLD:ALL]
    new_gram = overlap[OLD:ALL, OLD:ALL]
    second_weights = first_weights - small_dot(old_gram, first_weights)
    left_over = second_weights - small_dot(old_gram, second_weights)
    both = first_weights + second_weights
    both_t = flip(both)
    gram = new_gram - small_dot(flip(first_weights), both) - small_dot(both_t, left_over)
    inverse = lower_inverse(gram)
    mix = jnp.concatenate([-small_dot(inverse, both_t), inverse], axis=1)
    mix_t = flip(mix)
    mix_wide = jnp.concatenate([mix, jnp.zeros((NEW, LANES - ALL), F32)], axis=1)
    for k, piece in enumerate(split(mix_wide, 3)):
        for s in range(PARTS):
            weights[k * NEW : (k + 1) * NEW, s * LANES : (s + 1) * LANES] = piece

    conduct, drift, loss, capacity = cell_fields(
        region_ref, conductivity, damping, drift_speed, heat_capacity
    )
    shape = (ROWS, width)
    lane = lanes_of(shape)
    row = rows_of(shape)
    z_index = lane % NZ
    z_down, z_up = z_terms(conduct, z_index)
    low_half = lanes_of((1, LANES)) < NZ

    def face_conduct(ref, at_low):
        tile = jnp.concatenate([ref[r, ALL : ALL + 1, :] for r in range(HALF)], axis=0)
        turned = pltpu.roll(tile, NZ, 1)
        pair = [tile, turned] if at_low else [turned, tile]
        return jnp.concatenate(pair, axis=0)

    blank = jnp.zeros((ROWS, width - LANES), F32)
    before = jnp.concatenate([face_conduct(y_before, True), blank], axis=1)
    after = jnp.concatenate([blank, face_conduct(y_after, False)], axis=1)
    near_y = jnp.where(lane < NZ, before, pltpu.roll(conduct, NZ, 1))
    far_y = jnp.where(lane >= width - NZ, after, pltpu.roll(conduct, width - NZ, 1))
    x_line = [
        jnp.concatenate([ref[j, ALL : ALL + 1, :] for j in range(CHUNKS)], axis=1)
        for ref in (x_before, x_after)
    ]
    near_x = jnp.where(row == 0, x_line[0], pltpu.roll(conduct, 1, 0))
    far_x = jnp.where(row == ROWS - 1, x_line[1], pltpu.roll(conduct, ROWS - 1, 0))
    keep_coef = coef_writer(coef)
    y_down, y_up = 0.5 * (conduct + near_y), 0.5 * (conduct + far_y)
    x_down, x_up = 0.5 * (conduct + near_x), 0.5 * (conduct + far_x)
    keep_coef(0, x_down + drift)
    keep_coef(1, x_up)
    keep_coef(2, y_down)
    keep_coef(3, y_up)
    keep_coef(4, jnp.where(z_index == 0, 0.0, z_down))
    keep_coef(5, jnp.where(z_index == NZ - 1, 0.0, z_up))
    keep_coef(6, -(z_down + z_up + y_down + y_up + x_down + x_up + drift + loss))

    zero_rows = jnp.zeros((LANES - ALL, width), BF16)
    for stack in (first, second):
        for s in range(PARTS):
            stack[s * LANES + ALL : (s + 1) * LANES, :] = zero_rows

    def fill(stack, tiles):
        for j, tile in enumerate(tiles):
            for s, piece in enumerate(split(tile, PARTS)):
                stack[s * LANES : s * LANES + ALL, pl.ds(j * LANES, LANES)] = piece

    def product(stack):
        result = jnp.dot(weights[...], stack[...], preferred_element_type=F32)
        return result[0:NEW] + (result[NEW : 2 * NEW] + result[2 * NEW : 3 * NEW])

    def row_tiles(x):
        return [field_row((old[j], new[j]), x) for j in range(CHUNKS)]

    def keep(x, value):
        field[x + 1] = value
        for j in range(CHUNKS):
            basis[j, pl.ds(x, NEW, stride=ROWS), :] = value[:, j * LANES : (j + 1) * LANES]

    fill(first, row_tiles(0))

    def basis_step(i, carry):
        fill(second, row_tiles(2 * i + 1))
        keep(2 * i, product(first))
        fill(first, row_tiles(jnp.minimum(2 * i + 2, ROWS - 1)))
        keep(2 * i + 1, product(second))
        return carry

    lax.fori_loop(0, ROWS // 2, basis_step, 0)
    copies = [
        pltpu.make_async_copy(
            basis.at[j], basis_out.at[:, pl.ds(j * LANES, LANES)], sems.at[j]
        )
        for j in range(CHUNKS)
    ]
    for copy in copies:
        copy.start()

    for ref, place in ((x_before, 0), (x_after, ROWS + 1)):
        fill(first, [ref[j, 0:ALL, :] for j in range(CHUNKS)])
        field[place] = product(first)
    for ref, target, at_low in ((y_before, low_y, True), (y_after, high_y, False)):
        for g in range(HALF // CHUNKS):
            stack = first if g % 2 == 0 else second
            fill(stack, [ref[g * CHUNKS + j, 0:ALL, :] for j in range(CHUNKS)])
            value = product(stack)
            for j in range(CHUNKS):
                tile = value[:, j * LANES : (j + 1) * LANES]
                turned = pltpu.roll(tile, NZ, 1)
                r = g * CHUNKS + j
                target[r] = tile if at_low else turned
                target[r + HALF] = turned if at_low else tile

    def apply_step(x, carry):
        mid = [field[x + 1, :, j * LANES : (j + 1) * LANES] for j in range(CHUNKS)]
        swapped = [pltpu.roll(value, NZ, 1) for value in mid]
        for j in range(CHUNKS):
            here = slice(j * LANES, (j + 1) * LANES)
            before_j = swapped[j - 1] if j > 0 else low_y[x]
            after_j = swapped[j + 1] if j < CHUNKS - 1 else high_y[x]
            left = jnp.where(low_half, before_j, swapped[j])
            right = jnp.where(low_half, swapped[j], after_j)

            def scale(index):
                return coef[index * CHUNKS + j, pl.ds(x, 1), :]

            value = mid[j]
            result = (
                scale(0) * field[x, :, here]
                + scale(1) * field[x + 2, :, here]
                + scale(2) * left
                + scale(3) * right
                + scale(4) * pltpu.roll(value, 1, 1)
                + scale(5) * pltpu.roll(value, LANES - 1, 1)
                + scale(6) * value
            )
            applied[j, pl.ds(x, NEW, stride=ROWS), :] = result
        return carry

    lax.fori_loop(0, ROWS, apply_step, 0)
    more = [
        pltpu.make_async_copy(
            applied.at[j], applied_out.at[:, pl.ds(j * LANES, LANES)], sems.at[CHUNKS + j]
        )
        for j in range(CHUNKS)
    ]
    for copy in more:
        copy.start()

    outside = small_dot(left_over, flip(inverse))
    unit = jnp.where(
        lanes_of((NEW, NEW)) == rows_of((NEW, NEW)), 1.0, 0.0
    )
    columns = small_dot(moved, mix_t)
    stiff_block[0:OLD, :] = columns[0:OLD] - shifts[0] * outside
    stiff_block[OLD:ALL, :] = small_dot(mix, columns) - shifts[0] * unit
    stiff_row[...] = small_dot(mix, moved[:, 0:OLD]) - shifts[0] * flip(outside)
    columns = small_dot(massed, mix_t)
    capacity_block[0:OLD, :] = columns[0:OLD] + shifts[1] * outside
    capacity_block[OLD:ALL, :] = small_dot(mix, columns) + shifts[1] * unit
    sensor_block[...] = flip(small_dot(mix, sensed))
    source_block[...] = small_dot(mix, source)

    for copy in copies + more:
        copy.wait()


def all_sum(block):
    count_x = lax.axis_size("gx")
    count_y = lax.axis_size("gy")
    rows = block.shape[0] // count_x

    def swap(pieces, axis):
        return lax.all_to_all(pieces, axis, 0, 0)

    piece = jnp.sum(swap(block.reshape(count_x, rows, LANES), "gx"), axis=0)
    piece = jnp.sum(
        swap(jnp.broadcast_to(piece[None], (count_y, rows, LANES)), "gy"), axis=0
    )
    whole = swap(jnp.broadcast_to(piece[None], (count_x, rows, LANES)), "gx")
    return whole.reshape(block.shape)


def per_device(
    old_basis,
    new_block,
    source_matrix,
    region_map,
    conductivity,
    damping,
    drift_speed,
    heat_capacity,
    sensor_cells,
):
    width_x = old_basis.shape[1]
    width_yz = old_basis.shape[2]
    count_x = lax.axis_size("gx")
    count_y = lax.axis_size("gy")
    volume = 1.0 / (width_x * count_x * width_yz * count_y)
    index_x = lax.axis_index("gx")
    index_y = lax.axis_index("gy")
    old = old_basis.reshape(OLD * ROWS, width_yz)
    new = new_block.reshape(NEW * ROWS, width_yz)
    source = source_matrix.reshape(NEW * ROWS, width_yz)

    row_span = width_yz * count_y
    x_global = sensor_cells // row_span
    remainder = sensor_cells % row_span
    inside = (x_global // width_x == index_x) & (remainder // width_yz == index_y)
    places = jnp.where(
        inside, (x_global - index_x * width_x) * width_yz + remainder - index_y * width_yz, -1
    )
    shifts = jnp.stack(
        [
            6.0 * jnp.mean(conductivity) + jnp.mean(damping * heat_capacity) + jnp.mean(drift_speed),
            jnp.mean(heat_capacity),
        ]
    )
    edges = jnp.stack([index_x == count_x - 1, index_y == count_y - 1]).astype(jnp.int32)

    whole = pl.BlockSpec(memory_space=pltpu.VMEM)
    scalar = pl.BlockSpec(memory_space=pltpu.SMEM)
    hbm = pl.BlockSpec(memory_space=pl.ANY)
    params = pltpu.CompilerParams(vmem_limit_bytes=VMEM_LIMIT)

    def columns(rows):
        return [
            pl.BlockSpec((rows, LANES), functools.partial(lambda j, *_: (0, j), j))
            for j in range(CHUNKS)
        ]

    def shape(*sizes):
        return jax.ShapeDtypeStruct(sizes, F32)

    fields = [old] * CHUNKS + [new] * CHUNKS
    field_specs = columns(OLD * ROWS) + columns(NEW * ROWS)
    tables = (conductivity, damping, drift_speed, heat_capacity)

    y_top, y_low, x_top, x_low, coef = pl.pallas_call(
        pack_kernel,
        grid=(1,),
        out_shape=[
            shape(HALF, FACE, LANES),
            shape(HALF, FACE, LANES),
            shape(CHUNKS, XFACE, LANES),
            shape(CHUNKS, XFACE, LANES),
            shape(8 * CHUNKS, ROWS, LANES),
        ],
        in_specs=[whole] + [scalar] * 6 + field_specs,
        out_specs=[whole] * 5,
        compiler_params=params,
        name="pack",
    )(region_map, *tables, shifts, edges, *fields)

    def onward(value, axis):
        return lax.ppermute(value, axis, [(i, i + 1) for i in range(lax.axis_size(axis) - 1)])

    def backward(value, axis):
        return lax.ppermute(value, axis, [(i + 1, i) for i in range(lax.axis_size(axis) - 1)])

    y_before = onward(y_top, "gy")
    x_before = onward(x_top, "gx")
    y_after = backward(y_low, "gy")
    x_after = backward(x_low, "gx")

    stack_rows = 2 * LANES + 4 * ALL + 2 * NEW
    stack_width = GROUP * CHUNKS * LANES
    gram, sensed = pl.pallas_call(
        gram_kernel,
        grid=(1,),
        out_shape=[shape(stack_rows, 2 * LANES), shape(ALL, LANES)],
        in_specs=[scalar, whole] + field_specs + columns(NEW * ROWS),
        out_specs=[whole] * 2,
        scratch_shapes=[pltpu.VMEM((stack_rows, stack_width), BF16)] * 2,
        compiler_params=params,
        cost_estimate=pl.CostEstimate(
            flops=2 * stack_rows * 2 * LANES * width_x * width_yz,
            bytes_accessed=(ALL + NEW) * 4 * width_x * width_yz,
            transcendentals=0,
        ),
        name="gram",
    )(places, coef, *fields, *([source] * CHUNKS))

    face_width = (HALF + CHUNKS) * LANES
    partial = pl.pallas_call(
        face_kernel,
        out_shape=shape(2 * ALL, LANES),
        in_specs=[whole] * 6,
        out_specs=whole,
        scratch_shapes=[
            pltpu.VMEM((2 * ALL, face_width), BF16),
            pltpu.VMEM((2 * LANES, face_width), BF16),
        ],
        compiler_params=params,
        name="faces",
    )(gram, sensed, y_low, y_before, x_low, x_before)

    summed = all_sum(partial)

    results = pl.pallas_call(
        functools.partial(basis_kernel, volume),
        grid=(1,),
        out_shape=[
            shape(NEW * ROWS, width_yz),
            shape(NEW * ROWS, width_yz),
            shape(ALL, NEW),
            shape(NEW, OLD),
            shape(ALL, NEW),
            shape(16, NEW),
            shape(NEW, NEW),
        ],
        in_specs=[whole] + [scalar] * 5 + [whole] * 5 + field_specs,
        out_specs=[hbm, hbm] + [whole] * 5,
        scratch_shapes=[
            pltpu.VMEM((7 * CHUNKS, ROWS, LANES), F32),
            pltpu.VMEM((ROWS + 2, NEW, width_yz), F32),
            pltpu.VMEM((ROWS, NEW, LANES), F32),
            pltpu.VMEM((ROWS, NEW, LANES), F32),
            pltpu.VMEM((CHUNKS, NEW * ROWS, LANES), F32),
            pltpu.VMEM((CHUNKS, NEW * ROWS, LANES), F32),
            pltpu.VMEM((PARTS * LANES, width_yz), BF16),
            pltpu.VMEM((PARTS * LANES, width_yz), BF16),
            pltpu.VMEM((3 * NEW, PARTS * LANES), BF16),
            pltpu.SemaphoreType.DMA((2 * CHUNKS,)),
        ],
        compiler_params=params,
        name="basis",
    )(region_map, *tables, shifts, summed, y_before, y_after, x_before, x_after, *fields)
    return (
        results[0].reshape(new_block.shape),
        results[1].reshape(new_block.shape),
        *results[2:],
    )


def solution(mesh):
    in_specs = (
        P(None, "gx", "gy"),
        P(None, "gx", "gy"),
        P(None, "gx", "gy"),
        P("gx", "gy"),
        P(),
        P(),
        P(),
        P(),
        P(),
    )
    out_specs = (P(None, "gx", "gy"), P(None, "gx", "gy"), P(), P(), P(), P(), P())
    return jax.shard_map(
        per_device, mesh=mesh, in_specs=in_specs, out_specs=out_specs, check_vma=False
    )
```

```python
import functools

import jax
import jax.numpy as jnp
from jax import lax
from jax.experimental import pallas as pl
from jax.experimental.pallas import tpu as pltpu
from jax.sharding import PartitionSpec as P

NZ = 64
LANES = 128
OLD = 64
NEW = 32
ALL = OLD + NEW
ROWS = 32
CHUNKS = 4
HALF = ROWS // 2
GROUP = 4
PARTS = 3
FACE = ALL + 8
XFACE = ALL + 16
PAYLOAD = 2 * LANES
ALONG_X = ("x", "core")
ALONG_Y = ("z", "y")
F32 = jnp.float32
BF16 = jnp.bfloat16
HIGH = lax.Precision.HIGHEST
VMEM_LIMIT = 56 * 1024 * 1024


def position(axes):
    slow, fast = axes
    return lax.axis_index(slow) * lax.axis_size(fast) + lax.axis_index(fast)


def split(value, count):
    pieces = []
    for _ in range(count):
        piece = value.astype(BF16)
        pieces.append(piece)
        value = value - piece.astype(F32)
    return pieces


def lanes_of(shape):
    return lax.broadcasted_iota(jnp.int32, shape, len(shape) - 1)


def rows_of(shape):
    return lax.broadcasted_iota(jnp.int32, shape, 0)


def table_mean(table):
    total = table[0]
    for r in range(1, 8):
        total = total + table[r]
    return total * 0.125


def common_shifts(conductivity, damping, drift_speed, heat_capacity):
    loss = damping[0] * heat_capacity[0]
    for r in range(1, 8):
        loss = loss + damping[r] * heat_capacity[r]
    stiff = 6.0 * table_mean(conductivity) + table_mean(drift_speed) + loss * 0.125
    return stiff, table_mean(heat_capacity)


def row_copies(old, new, rows, sems, x):
    return [
        pltpu.make_async_copy(old.at[:, x, :], rows.at[x, pl.ds(0, OLD), :], sems.at[x]),
        pltpu.make_async_copy(new.at[:, x, :], rows.at[x, pl.ds(OLD, NEW), :], sems.at[x]),
    ]


def cell_fields(region_ref, conductivity, damping, drift_speed, heat_capacity):
    region = region_ref[...]
    conduct = jnp.zeros(region.shape, F32)
    drift = jnp.zeros(region.shape, F32)
    loss = jnp.zeros(region.shape, F32)
    capacity = jnp.zeros(region.shape, F32)
    for r in range(8):
        here = region == r
        conduct = jnp.where(here, conductivity[r], conduct)
        drift = jnp.where(here, drift_speed[r], drift)
        loss = jnp.where(here, damping[r] * heat_capacity[r], loss)
        capacity = jnp.where(here, heat_capacity[r], capacity)
    return conduct, drift, loss, capacity


def z_terms(conduct, z_index):
    low_z = jnp.where(z_index == 0, 0.0, pltpu.roll(conduct, 1, 1))
    high_z = jnp.where(z_index == NZ - 1, 0.0, pltpu.roll(conduct, conduct.shape[1] - 1, 1))
    return 0.5 * (conduct + low_z), 0.5 * (conduct + high_z)


def coef_writer(coef):
    def keep_coef(index, value):
        for j in range(CHUNKS):
            coef[index * CHUNKS + j] = value[:, j * LANES : (j + 1) * LANES]

    return keep_coef


def pack_kernel(
    region_ref,
    conductivity,
    damping,
    drift_speed,
    heat_capacity,
    old,
    new,
    old_first,
    old_last,
    new_first,
    new_last,
    y_top,
    y_low,
    x_top,
    x_low,
    coef,
    sems,
):
    width = CHUNKS * LANES
    copies = []
    for out, row, base in ((x_top, ROWS - 1, 0), (x_low, 0, 2 * CHUNKS)):
        for j in range(CHUNKS):
            here = pl.ds(j * LANES, LANES)
            for field, start, count, shift in ((old, 0, OLD, 0), (new, OLD, NEW, CHUNKS)):
                copies.append(
                    pltpu.make_async_copy(
                        field.at[:, row, here],
                        out.at[j, pl.ds(start, count), :],
                        sems.at[base + shift + j],
                    )
                )
    for copy in copies:
        copy.start()
    conduct, drift, loss, capacity = cell_fields(
        region_ref, conductivity, damping, drift_speed, heat_capacity
    )
    low_half = lanes_of((1, LANES)) < NZ

    def tail(rows, value):
        return jnp.broadcast_to(value, (rows, LANES))

    def turned(ref, f, x):
        return jnp.transpose(ref[f : f + 8, x : x + 8, :], (1, 0, 2))

    for first, last, start, count in (
        (old_first, old_last, 0, OLD),
        (new_first, new_last, OLD, NEW),
    ):
        for f in range(0, count, 8):
            for x in range(0, HALF, 8):
                at = (slice(x, x + 8), slice(start + f, start + f + 8), slice(None))
                near, far = turned(last, f, x), turned(last, f, x + HALF)
                y_top[at] = jnp.where(low_half[None], pltpu.roll(near, NZ, 2), far)
                near, far = turned(first, f, x), turned(first, f, x + HALF)
                y_low[at] = jnp.where(low_half[None], near, pltpu.roll(far, NZ, 2))
    near, far = conduct[:HALF, width - LANES :], conduct[HALF:, width - LANES :]
    top_line = jnp.where(low_half, pltpu.roll(near, NZ, 1), far)
    near, far = conduct[:HALF, :LANES], conduct[HALF:, :LANES]
    low_line = jnp.where(low_half, near, pltpu.roll(far, NZ, 1))
    for r in range(HALF):
        y_top[r, ALL:FACE, :] = tail(8, top_line[r : r + 1])
        y_low[r, ALL:FACE, :] = tail(8, low_line[r : r + 1])
    for j in range(CHUNKS):
        here = slice(j * LANES, (j + 1) * LANES)
        for out, row in ((x_top, ROWS - 1), (x_low, 0)):
            out[j, ALL : ALL + 8, :] = tail(8, conduct[row : row + 1, here])
            out[j, ALL + 8 : XFACE, :] = tail(8, drift[row : row + 1, here])

    shape = (ROWS, width)
    lane = lanes_of(shape)
    row = rows_of(shape)
    z_index = lane % NZ
    z_down, z_up = z_terms(conduct, z_index)
    half = 0.5 * conduct
    from_low_y = 0.5 * (conduct + pltpu.roll(conduct, NZ, 1))
    from_high_y = 0.5 * (conduct + pltpu.roll(conduct, width - NZ, 1))
    from_low_x = 0.5 * (conduct + pltpu.roll(conduct, 1, 0))
    from_high_x = 0.5 * (conduct + pltpu.roll(conduct, ROWS - 1, 0))
    y_down = jnp.where(lane < NZ, 0.0, from_low_y)
    y_up = jnp.where(lane >= width - NZ, 0.0, from_high_y)
    x_down = jnp.where(row == 0, 0.0, from_low_x)
    x_up = jnp.where(row == ROWS - 1, 0.0, from_high_x)
    pull = jnp.where(row == 0, 0.0, drift)
    x_last = jnp.where(position(ALONG_X) == lax.axis_size(ALONG_X) - 1, 1.0, 0.0)
    y_last = jnp.where(position(ALONG_Y) == lax.axis_size(ALONG_Y) - 1, 1.0, 0.0)
    shifts = common_shifts(conductivity, damping, drift_speed, heat_capacity)
    border = jnp.where(row == ROWS - 1, half * x_last, 0.0) + jnp.where(
        lane >= width - NZ, half * y_last, 0.0
    )
    keep_coef = coef_writer(coef)
    total = z_down + z_up + y_down + y_up + x_down + x_up + pull + loss + border
    keep_coef(0, x_down + pull)
    keep_coef(1, x_up)
    keep_coef(2, y_down)
    keep_coef(3, y_up)
    keep_coef(4, jnp.where(z_index == 0, 0.0, z_down))
    keep_coef(5, jnp.where(z_index == NZ - 1, 0.0, z_up))
    keep_coef(6, shifts[0] - total)
    keep_coef(7, capacity - shifts[1])
    for copy in copies:
        copy.wait()


def gram_kernel(sensor_cells, coef, old, new, source, out, sensed, stack, rows, sources, sems):
    width = CHUNKS * LANES

    def incoming(x):
        return row_copies(old, new, rows, sems, x) + [
            pltpu.make_async_copy(source.at[:, x, :], sources.at[x], sems.at[x])
        ]

    def begin(x, carry):
        for copy in incoming(x):
            copy.start()
        return carry

    lax.fori_loop(0, ROWS, begin, 0)
    low_half = lanes_of((1, LANES)) < NZ
    zero_rows = jnp.zeros((LANES - ALL, stack.shape[1]), BF16)
    stack[ALL:LANES, :] = zero_rows
    stack[LANES + ALL : 2 * LANES, :] = zero_rows
    out[...] = jnp.zeros(out.shape, F32)

    def arrive(x):
        for copy in incoming(x):
            copy.wait()

    def fill(group):
        for r in range(GROUP):
            x = group * GROUP + r
            if r < GROUP - 1:
                arrive(x + 1)
            else:
                pl.when(x + 1 < ROWS)(lambda: arrive(x + 1))
            below = jnp.maximum(x - 1, 0)
            above = jnp.minimum(x + 1, ROWS - 1)
            mid = [rows[x, :, j * LANES : (j + 1) * LANES] for j in range(CHUNKS)]
            swapped = [pltpu.roll(value, NZ, 1) for value in mid]
            for j in range(CHUNKS):
                here = slice(j * LANES, (j + 1) * LANES)
                left = jnp.where(low_half, swapped[max(j - 1, 0)], swapped[j])
                right = jnp.where(low_half, swapped[j], swapped[min(j + 1, CHUNKS - 1)])

                def scale(index):
                    return coef[index * CHUNKS + j, pl.ds(x, 1), :]

                value = mid[j]
                moved = (
                    scale(0) * rows[below, :, here]
                    + scale(1) * rows[above, :, here]
                    + scale(2) * left
                    + scale(3) * right
                    + scale(4) * pltpu.roll(value, 1, 1)
                    + scale(5) * pltpu.roll(value, LANES - 1, 1)
                    + scale(6) * value
                )
                at = pl.ds((r * CHUNKS + j) * LANES, LANES)
                high, low = split(value, 2)
                stack[0:ALL, at] = high
                stack[LANES : LANES + ALL, at] = low
                base = 2 * LANES
                for item in (moved, scale(7) * value):
                    high, low = split(item, 2)
                    stack[base : base + ALL, at] = high
                    stack[base + ALL : base + 2 * ALL, at] = low
                    base += 2 * ALL
                high, low = split(sources[x, :, here], 2)
                stack[base : base + NEW, at] = high
                stack[base + NEW : base + 2 * NEW, at] = low

    arrive(0)

    def step(i, carry):
        fill(i)
        out[...] += lax.dot_general(
            stack[...],
            stack[0 : 2 * LANES, :],
            (((1,), (1,)), ((), ())),
            preferred_element_type=F32,
        )
        return carry

    lax.fori_loop(0, ROWS // GROUP, step, 0)

    lane = lanes_of((ALL, LANES))
    sensed[...] = jnp.zeros(sensed.shape, F32)
    row_span = width * lax.axis_size(ALONG_Y)
    index_x, index_y = position(ALONG_X), position(ALONG_Y)

    def sense(p, carry):
        cell = sensor_cells[p]
        x_global = cell // row_span
        remainder = cell % row_span
        inside = (x_global // ROWS == index_x) & (remainder // width == index_y)

        @pl.when(inside)
        def _():
            x = x_global % ROWS
            column = remainder % width
            found = jnp.zeros((ALL, LANES), F32)
            for j in range(CHUNKS):
                value = rows[x, :, j * LANES : (j + 1) * LANES]
                found = jnp.where(lane == column - j * LANES, value, found)
            picked = jnp.sum(found, axis=1, keepdims=True)
            sensed[...] = jnp.where(lane == p, picked, sensed[...])

        return carry

    lax.fori_loop(0, sensor_cells.shape[0], sense, 0)


def fold(block, rows):
    return (
        block[0:rows, 0:LANES]
        + block[rows : 2 * rows, 0:LANES]
        + (block[0:rows, LANES:] + block[rows : 2 * rows, LANES:])
    )


def face_kernel(gram, sensed, y_own, y_near, x_own, x_near, out, diffs, scaled):
    tiles = HALF + CHUNKS
    zero_rows = jnp.zeros((LANES - ALL, tiles * LANES), BF16)
    scaled[ALL:LANES, :] = zero_rows
    scaled[LANES + ALL : 2 * LANES, :] = zero_rows
    for t in range(tiles):
        at = pl.ds(t * LANES, LANES)
        if t < HALF:
            own, near = y_own.at[t], y_near.at[t]
        else:
            own, near = x_own.at[t - HALF], x_near.at[t - HALF]
        value = own[0:ALL, :]
        diff = value - near[0:ALL, :]
        edge = 0.5 * (own[ALL : ALL + 1, :] + near[ALL : ALL + 1, :])
        weighted = edge * diff
        if t >= HALF:
            weighted = weighted + own[ALL + 8 : ALL + 9, :] * value
        high, low = split(diff, 2)
        diffs[0:ALL, at] = high
        diffs[ALL : 2 * ALL, at] = low
        high, low = split(weighted, 2)
        scaled[0:ALL, at] = high
        scaled[LANES : LANES + ALL, at] = low
    faces = lax.dot_general(
        diffs[...], scaled[...], (((1,), (1,)), ((), ())), preferred_element_type=F32
    )
    base = 2 * LANES
    overlap = (
        gram[0:ALL, 0:LANES]
        + gram[0:ALL, LANES:]
        + (gram[LANES : LANES + ALL, 0:LANES] + gram[LANES : LANES + ALL, LANES:])
    )
    moved = fold(gram[base : base + 2 * ALL, :], ALL) - fold(faces, ALL)
    base += 2 * ALL
    massed = fold(gram[base : base + 2 * ALL, :], ALL)
    base += 2 * ALL
    source = fold(gram[base : base + 2 * NEW, :], NEW)
    source = jnp.concatenate([source, jnp.zeros((LANES - NEW, LANES), F32)], axis=0).T
    source = pltpu.roll(source[0:ALL, :], ALL, 1)
    lane = lanes_of((ALL, LANES))
    row = rows_of((ALL, LANES))
    diagonal = jnp.sum(jnp.where(lane == row, massed, 0.0), axis=1, keepdims=True)
    upper = jnp.where(row >= lane, overlap, massed)
    out[0:ALL, :] = jnp.where(lane < ALL, upper, source)
    extra = jnp.where(lane == ALL + 16, diagonal, pltpu.roll(sensed[...], ALL, 1))
    out[ALL : 2 * ALL, :] = jnp.where(lane < ALL, moved, extra)
    out[2 * ALL : PAYLOAD, :] = jnp.zeros((PAYLOAD - 2 * ALL, LANES), F32)


def small_dot(left, right):
    return lax.dot_general(
        left, right, (((1,), (0,)), ((), ())), preferred_element_type=F32, precision=HIGH
    )


def flip(block):
    rows, columns = block.shape
    if rows < LANES:
        block = jnp.concatenate([block, jnp.zeros((LANES - rows, columns), F32)], axis=0)
    if columns < LANES:
        block = jnp.concatenate([block, jnp.zeros((LANES, LANES - columns), F32)], axis=1)
    return block.T[0:columns, 0:rows]


def lower_inverse(gram):
    shape = (NEW, LANES)
    lane, row = lanes_of(shape), rows_of(shape)
    work = jnp.concatenate(
        [gram, jnp.zeros((NEW, LANES - NEW), F32)], axis=1
    ) + jnp.where(lane == row + NEW, 1.0, 0.0)
    for k in range(NEW):
        pivot = work[k : k + 1, k : k + 1]
        line = work[k : k + 1, :] / pivot
        factor = jnp.where(row[:, 0:1] > k, work[:, k : k + 1], 0.0)
        work = work - factor * line
    pivots = jnp.sum(jnp.where(lane == row, work, 0.0), axis=1, keepdims=True)
    return (work / jnp.sqrt(pivots))[:, NEW : 2 * NEW]


def basis_kernel(
    volume,
    region_ref,
    conductivity,
    damping,
    drift_speed,
    heat_capacity,
    summed,
    y_before,
    y_after,
    x_before,
    x_after,
    old,
    new,
    basis_out,
    applied_out,
    stiff_block,
    stiff_row,
    capacity_block,
    sensor_block,
    source_block,
    rows,
    coef,
    field,
    applied,
    low_y,
    high_y,
    first,
    second,
    weights,
    sems,
    basis_sems,
    applied_sems,
):
    width = CHUNKS * LANES

    def begin(x, carry):
        for copy in row_copies(old, new, rows, sems, x):
            copy.start()
        return carry

    lax.fori_loop(0, ROWS, begin, 0)
    shifts = common_shifts(conductivity, damping, drift_speed, heat_capacity)

    lane = lanes_of((ALL, LANES))
    row = rows_of((ALL, LANES))
    top = summed[0:ALL, :] * volume
    bottom = summed[ALL : 2 * ALL, :] * volume
    upper = jnp.where(lane < ALL, top, 0.0)
    low_part = jnp.where(lane <= row, upper, 0.0)
    high_part = jnp.where(lane > row, upper, 0.0)
    diagonal = jnp.where(lane == row, low_part, 0.0)
    overlap = (low_part - diagonal)[:, 0:ALL] + flip(low_part[:, 0:ALL])
    mass_diagonal = jnp.where(lane == row, bottom[:, ALL + 16 : ALL + 17], 0.0)
    massed = (high_part + mass_diagonal)[:, 0:ALL] + flip(high_part[:, 0:ALL])
    moved = flip(bottom[:, 0:ALL])
    source = top[:, ALL:LANES]
    sensed = summed[ALL : 2 * ALL, ALL : ALL + 16]

    old_gram = overlap[0:OLD, 0:OLD]
    first_weights = overlap[0:OLD, OLD:ALL]
    new_gram = overlap[OLD:ALL, OLD:ALL]
    second_weights = first_weights - small_dot(old_gram, first_weights)
    left_over = second_weights - small_dot(old_gram, second_weights)
    both = first_weights + second_weights
    both_t = flip(both)
    gram = new_gram - small_dot(flip(first_weights), both) - small_dot(both_t, left_over)
    inverse = lower_inverse(gram)
    mix = jnp.concatenate([-small_dot(inverse, both_t), inverse], axis=1)
    mix_t = flip(mix)
    mix_wide = jnp.concatenate([mix, jnp.zeros((NEW, LANES - ALL), F32)], axis=1)
    for k, piece in enumerate(split(mix_wide, 3)):
        for s in range(PARTS):
            weights[k * NEW : (k + 1) * NEW, s * LANES : (s + 1) * LANES] = piece

    conduct, drift, loss, capacity = cell_fields(
        region_ref, conductivity, damping, drift_speed, heat_capacity
    )
    shape = (ROWS, width)
    lane = lanes_of(shape)
    row = rows_of(shape)
    z_index = lane % NZ
    z_down, z_up = z_terms(conduct, z_index)
    low_half = lanes_of((1, LANES)) < NZ

    def face_conduct(ref, at_low):
        tile = jnp.concatenate([ref[r, ALL : ALL + 1, :] for r in range(HALF)], axis=0)
        turned = pltpu.roll(tile, NZ, 1)
        pair = [tile, turned] if at_low else [turned, tile]
        return jnp.concatenate(pair, axis=0)

    blank = jnp.zeros((ROWS, width - LANES), F32)
    before = jnp.concatenate([face_conduct(y_before, True), blank], axis=1)
    after = jnp.concatenate([blank, face_conduct(y_after, False)], axis=1)
    near_y = jnp.where(lane < NZ, before, pltpu.roll(conduct, NZ, 1))
    far_y = jnp.where(lane >= width - NZ, after, pltpu.roll(conduct, width - NZ, 1))
    x_line = [
        jnp.concatenate([ref[j, ALL : ALL + 1, :] for j in range(CHUNKS)], axis=1)
        for ref in (x_before, x_after)
    ]
    near_x = jnp.where(row == 0, x_line[0], pltpu.roll(conduct, 1, 0))
    far_x = jnp.where(row == ROWS - 1, x_line[1], pltpu.roll(conduct, ROWS - 1, 0))
    keep_coef = coef_writer(coef)
    y_down, y_up = 0.5 * (conduct + near_y), 0.5 * (conduct + far_y)
    x_down, x_up = 0.5 * (conduct + near_x), 0.5 * (conduct + far_x)
    keep_coef(0, x_down + drift)
    keep_coef(1, x_up)
    keep_coef(2, y_down)
    keep_coef(3, y_up)
    keep_coef(4, jnp.where(z_index == 0, 0.0, z_down))
    keep_coef(5, jnp.where(z_index == NZ - 1, 0.0, z_up))
    keep_coef(6, -(z_down + z_up + y_down + y_up + x_down + x_up + drift + loss))

    zero_rows = jnp.zeros((LANES - ALL, width), BF16)
    for stack in (first, second):
        for s in range(PARTS):
            stack[s * LANES + ALL : (s + 1) * LANES, :] = zero_rows

    def fill(stack, tiles):
        for j, tile in enumerate(tiles):
            for s, piece in enumerate(split(tile, PARTS)):
                stack[s * LANES : s * LANES + ALL, pl.ds(j * LANES, LANES)] = piece

    def product(stack):
        result = jnp.dot(weights[...], stack[...], preferred_element_type=F32)
        return result[0:NEW] + (result[NEW : 2 * NEW] + result[2 * NEW : 3 * NEW])

    for ref, place in ((x_before, 0), (x_after, ROWS + 1)):
        fill(first, [ref[j, 0:ALL, :] for j in range(CHUNKS)])
        field[place] = product(first)
    for ref, target, at_low in ((y_before, low_y, True), (y_after, high_y, False)):
        for g in range(HALF // CHUNKS):
            stack = first if g % 2 == 0 else second
            fill(stack, [ref[g * CHUNKS + j, 0:ALL, :] for j in range(CHUNKS)])
            value = product(stack)
            for j in range(CHUNKS):
                tile = value[:, j * LANES : (j + 1) * LANES]
                turned = pltpu.roll(tile, NZ, 1)
                r = g * CHUNKS + j
                target[r] = tile if at_low else turned
                target[r + HALF] = turned if at_low else tile

    def load(stack, x):
        for copy in row_copies(old, new, rows, sems, x):
            copy.wait()
        fill(stack, [rows[x, :, j * LANES : (j + 1) * LANES] for j in range(CHUNKS)])

    def basis_copy(x):
        return pltpu.make_async_copy(field.at[x + 1], basis_out.at[:, x, :], basis_sems.at[x])

    def applied_copy(x):
        return pltpu.make_async_copy(applied.at[x], applied_out.at[:, x, :], applied_sems.at[x])

    def keep(x, stack):
        field[x + 1] = product(stack)
        basis_copy(x).start()

    def apply(x):
        mid = [field[x + 1, :, j * LANES : (j + 1) * LANES] for j in range(CHUNKS)]
        swapped = [pltpu.roll(value, NZ, 1) for value in mid]
        for j in range(CHUNKS):
            here = slice(j * LANES, (j + 1) * LANES)
            before_j = swapped[j - 1] if j > 0 else low_y[x]
            after_j = swapped[j + 1] if j < CHUNKS - 1 else high_y[x]
            left = jnp.where(low_half, before_j, swapped[j])
            right = jnp.where(low_half, swapped[j], after_j)

            def scale(index):
                return coef[index * CHUNKS + j, pl.ds(x, 1), :]

            value = mid[j]
            applied[x, :, here] = (
                scale(0) * field[x, :, here]
                + scale(1) * field[x + 2, :, here]
                + scale(2) * left
                + scale(3) * right
                + scale(4) * pltpu.roll(value, 1, 1)
                + scale(5) * pltpu.roll(value, LANES - 1, 1)
                + scale(6) * value
            )
        applied_copy(x).start()

    load(first, 0)
    load(second, 1)
    keep(0, first)

    def step(i, carry):
        x = 2 * i + 1
        keep(x, second)
        load(first, x + 1)
        apply(x - 1)
        keep(x + 1, first)
        load(second, x + 2)
        apply(x)
        return carry

    lax.fori_loop(0, ROWS // 2 - 1, step, 0)
    keep(ROWS - 1, second)
    apply(ROWS - 2)
    apply(ROWS - 1)

    outside = small_dot(left_over, flip(inverse))
    unit = jnp.where(
        lanes_of((NEW, NEW)) == rows_of((NEW, NEW)), 1.0, 0.0
    )
    columns = small_dot(moved, mix_t)
    stiff_columns = columns[0:OLD] - shifts[0] * outside
    stiff_rest = small_dot(mix, columns) - shifts[0] * unit
    stiff_block[...] = flip(jnp.concatenate([stiff_columns, stiff_rest], axis=0))
    stiff_row[...] = small_dot(mix, moved[:, 0:OLD]) - shifts[0] * flip(outside)
    columns = small_dot(massed, mix_t)
    mass_columns = columns[0:OLD] + shifts[1] * outside
    mass_rest = small_dot(mix, columns) + shifts[1] * unit
    capacity_block[...] = flip(jnp.concatenate([mass_columns, mass_rest], axis=0))
    sensor_block[...] = flip(small_dot(mix, sensed))
    source_block[...] = small_dot(mix, source)

    def finish(x, carry):
        basis_copy(x).wait()
        applied_copy(x).wait()
        return carry

    lax.fori_loop(0, ROWS, finish, 0)


def swap(pieces, axes):
    return lax.all_to_all(pieces, axes, 0, 0)


def spread(block, axes):
    count = lax.axis_size(axes)
    return jnp.sum(swap(block.reshape(count, -1, LANES), axes), axis=0)


def copies_of(piece, axes):
    return swap(jnp.broadcast_to(piece[None], (lax.axis_size(axes), *piece.shape)), axes)


def gathered(piece, axes):
    return copies_of(piece, axes).reshape(-1, LANES)


def all_sum(block):
    inner, outer = ("core", "z"), ("x", "y")
    piece = spread(block, inner)
    piece = jnp.sum(copies_of(piece, outer), axis=0)
    return gathered(piece, inner)


def per_device(
    old_basis,
    new_block,
    source_matrix,
    region_map,
    conductivity,
    damping,
    drift_speed,
    heat_capacity,
    sensor_cells,
):
    width_x = old_basis.shape[1]
    width_yz = old_basis.shape[2]
    count_x = lax.axis_size(ALONG_X)
    count_y = lax.axis_size(ALONG_Y)
    volume = 1.0 / (width_x * count_x * width_yz * count_y)
    whole = pl.BlockSpec(memory_space=pltpu.VMEM)
    scalar = pl.BlockSpec(memory_space=pltpu.SMEM)
    hbm = pl.BlockSpec(memory_space=pl.ANY)
    params = pltpu.CompilerParams(vmem_limit_bytes=VMEM_LIMIT)

    def shape(*sizes):
        return jax.ShapeDtypeStruct(sizes, F32)

    def column(count, j):
        return pl.BlockSpec((count, ROWS, LANES), lambda *_: (0, 0, j))

    tables = (conductivity, damping, drift_speed, heat_capacity)

    y_top, y_low, x_top, x_low, coef = pl.pallas_call(
        pack_kernel,
        grid=(1,),
        out_shape=[
            shape(HALF, FACE, LANES),
            shape(HALF, FACE, LANES),
            shape(CHUNKS, XFACE, LANES),
            shape(CHUNKS, XFACE, LANES),
            shape(8 * CHUNKS, ROWS, LANES),
        ],
        in_specs=[whole]
        + [scalar] * 4
        + [hbm] * 2
        + [column(OLD, 0), column(OLD, CHUNKS - 1), column(NEW, 0), column(NEW, CHUNKS - 1)],
        out_specs=[whole] * 5,
        scratch_shapes=[pltpu.SemaphoreType.DMA((4 * CHUNKS,))],
        compiler_params=params,
        name="pack",
    )(
        region_map,
        *tables,
        old_basis,
        new_block,
        old_basis,
        old_basis,
        new_block,
        new_block,
    )

    def onward(value, axis):
        return lax.ppermute(value, axis, [(i, i + 1) for i in range(lax.axis_size(axis) - 1)])

    def backward(value, axis):
        return lax.ppermute(value, axis, [(i + 1, i) for i in range(lax.axis_size(axis) - 1)])

    y_before = onward(y_top, ALONG_Y)
    x_before = onward(x_top, ALONG_X)
    y_after = backward(y_low, ALONG_Y)
    x_after = backward(x_low, ALONG_X)

    stack_rows = 2 * LANES + 4 * ALL + 2 * NEW
    stack_width = GROUP * CHUNKS * LANES
    gram, sensed = pl.pallas_call(
        gram_kernel,
        out_shape=[shape(stack_rows, 2 * LANES), shape(ALL, LANES)],
        in_specs=[scalar, whole] + [hbm] * 3,
        out_specs=[whole] * 2,
        scratch_shapes=[
            pltpu.VMEM((stack_rows, stack_width), BF16),
            pltpu.VMEM((ROWS, ALL, width_yz), F32),
            pltpu.VMEM((ROWS, NEW, width_yz), F32),
            pltpu.SemaphoreType.DMA((ROWS,)),
        ],
        compiler_params=params,
        cost_estimate=pl.CostEstimate(
            flops=2 * stack_rows * 2 * LANES * width_x * width_yz,
            bytes_accessed=(ALL + NEW) * 4 * width_x * width_yz,
            transcendentals=0,
        ),
        name="gram",
    )(sensor_cells, coef, old_basis, new_block, source_matrix)
    y_before, y_after, x_before, x_after, gram = lax.optimization_barrier(
        (y_before, y_after, x_before, x_after, gram)
    )

    face_width = (HALF + CHUNKS) * LANES
    partial = pl.pallas_call(
        face_kernel,
        out_shape=shape(PAYLOAD, LANES),
        in_specs=[whole] * 6,
        out_specs=whole,
        scratch_shapes=[
            pltpu.VMEM((2 * ALL, face_width), BF16),
            pltpu.VMEM((2 * LANES, face_width), BF16),
        ],
        compiler_params=params,
        name="faces",
    )(gram, sensed, y_low, y_before, x_low, x_before)

    summed = all_sum(partial)

    results = pl.pallas_call(
        functools.partial(basis_kernel, volume),
        out_shape=[
            shape(*new_block.shape),
            shape(*new_block.shape),
            shape(NEW, ALL),
            shape(NEW, OLD),
            shape(NEW, ALL),
            shape(16, NEW),
            shape(NEW, NEW),
        ],
        in_specs=[whole] + [scalar] * 4 + [whole] * 5 + [hbm] * 2,
        out_specs=[hbm, hbm] + [whole] * 5,
        scratch_shapes=[
            pltpu.VMEM((ROWS, ALL, width_yz), F32),
            pltpu.VMEM((7 * CHUNKS, ROWS, LANES), F32),
            pltpu.VMEM((ROWS + 2, NEW, width_yz), F32),
            pltpu.VMEM((ROWS, NEW, width_yz), F32),
            pltpu.VMEM((ROWS, NEW, LANES), F32),
            pltpu.VMEM((ROWS, NEW, LANES), F32),
            pltpu.VMEM((PARTS * LANES, width_yz), BF16),
            pltpu.VMEM((PARTS * LANES, width_yz), BF16),
            pltpu.VMEM((3 * NEW, PARTS * LANES), BF16),
            pltpu.SemaphoreType.DMA((ROWS,)),
            pltpu.SemaphoreType.DMA((ROWS,)),
            pltpu.SemaphoreType.DMA((ROWS,)),
        ],
        compiler_params=params,
        name="basis",
    )(
        region_map,
        *tables,
        summed,
        y_before,
        y_after,
        x_before,
        x_after,
        old_basis,
        new_block,
    )
    basis, applied, stiff_block, stiff_row, capacity_block, sensor_block, source_block = results
    return (
        basis,
        applied,
        stiff_block.T,
        stiff_row,
        capacity_block.T,
        sensor_block,
        source_block,
    )


def solution(mesh):
    mesh = jax.sharding.Mesh(mesh.devices.reshape(4, 2, 8, 4), ALONG_X + ALONG_Y)
    fields = P(None, ALONG_X, ALONG_Y)
    in_specs = (fields, fields, fields, P(ALONG_X, ALONG_Y), P(), P(), P(), P(), P())
    out_specs = (fields, fields, P(), P(), P(), P(), P())
    return jax.shard_map(
        per_device, mesh=mesh, in_specs=in_specs, out_specs=out_specs, check_vma=False
    )
```

```python
import functools

import jax
import jax.numpy as jnp
from jax import lax
from jax.experimental import pallas as pl
from jax.experimental.pallas import tpu as pltpu
from jax.sharding import PartitionSpec as P

NZ = 64
LANES = 128
OLD = 64
NEW = 32
ALL = OLD + NEW
ROWS = 32
CHUNKS = 4
HALF = ROWS // 2
GROUP = 4
PARTS = 3
FACE = ALL + 8
XFACE = ALL + 16
PAYLOAD = 2 * LANES
ALONG_X = ("x", "core")
ALONG_Y = ("z", "y")
F32 = jnp.float32
BF16 = jnp.bfloat16
HIGH = lax.Precision.HIGHEST
VMEM_LIMIT = 56 * 1024 * 1024


def position(axes):
    slow, fast = axes
    return lax.axis_index(slow) * lax.axis_size(fast) + lax.axis_index(fast)


def split(value, count):
    pieces = []
    for _ in range(count):
        piece = value.astype(BF16)
        pieces.append(piece)
        value = value - piece.astype(F32)
    return pieces


def lanes_of(shape):
    return lax.broadcasted_iota(jnp.int32, shape, len(shape) - 1)


def rows_of(shape):
    return lax.broadcasted_iota(jnp.int32, shape, 0)


def table_mean(table):
    total = table[0]
    for r in range(1, 8):
        total = total + table[r]
    return total * 0.125


def common_shifts(conductivity, damping, drift_speed, heat_capacity):
    loss = damping[0] * heat_capacity[0]
    for r in range(1, 8):
        loss = loss + damping[r] * heat_capacity[r]
    stiff = 6.0 * table_mean(conductivity) + table_mean(drift_speed) + loss * 0.125
    return stiff, table_mean(heat_capacity)


def turn(source, target, start, shift, fields, base):
    for f in range(0, fields, 8):
        for j in range(CHUNKS):
            here = slice(j * LANES, (j + 1) * LANES)
            tile = source[f : f + 8, pl.ds(start, 8), here]
            target[pl.ds(start + shift, 8), base + f : base + f + 8, here] = jnp.transpose(
                tile, (1, 0, 2)
            )


def turn_back(source, target, start, shift, fields):
    for f in range(0, fields, 8):
        for j in range(CHUNKS):
            here = slice(j * LANES, (j + 1) * LANES)
            tile = source[pl.ds(start + shift, 8), f : f + 8, here]
            target[f : f + 8, pl.ds(start, 8), here] = jnp.transpose(tile, (1, 0, 2))


def cell_fields(region_ref, conductivity, damping, drift_speed, heat_capacity):
    region = region_ref[...]
    conduct = jnp.zeros(region.shape, F32)
    drift = jnp.zeros(region.shape, F32)
    loss = jnp.zeros(region.shape, F32)
    capacity = jnp.zeros(region.shape, F32)
    for r in range(8):
        here = region == r
        conduct = jnp.where(here, conductivity[r], conduct)
        drift = jnp.where(here, drift_speed[r], drift)
        loss = jnp.where(here, damping[r] * heat_capacity[r], loss)
        capacity = jnp.where(here, heat_capacity[r], capacity)
    return conduct, drift, loss, capacity


def z_terms(conduct, z_index):
    low_z = jnp.where(z_index == 0, 0.0, pltpu.roll(conduct, 1, 1))
    high_z = jnp.where(z_index == NZ - 1, 0.0, pltpu.roll(conduct, conduct.shape[1] - 1, 1))
    return 0.5 * (conduct + low_z), 0.5 * (conduct + high_z)


def coef_writer(coef):
    def keep_coef(index, value):
        for j in range(CHUNKS):
            coef[index * CHUNKS + j] = value[:, j * LANES : (j + 1) * LANES]

    return keep_coef


def pack_kernel(
    region_ref,
    conductivity,
    damping,
    drift_speed,
    heat_capacity,
    old,
    new,
    old_first,
    old_last,
    new_first,
    new_last,
    y_top,
    y_low,
    x_top,
    x_low,
    coef,
    sems,
):
    width = CHUNKS * LANES
    copies = []
    for out, row, base in ((x_top, ROWS - 1, 0), (x_low, 0, 2 * CHUNKS)):
        for j in range(CHUNKS):
            here = pl.ds(j * LANES, LANES)
            for field, start, count, shift in ((old, 0, OLD, 0), (new, OLD, NEW, CHUNKS)):
                copies.append(
                    pltpu.make_async_copy(
                        field.at[:, row, here],
                        out.at[j, pl.ds(start, count), :],
                        sems.at[base + shift + j],
                    )
                )
    for copy in copies:
        copy.start()
    conduct, drift, loss, capacity = cell_fields(
        region_ref, conductivity, damping, drift_speed, heat_capacity
    )
    low_half = lanes_of((1, LANES)) < NZ

    def tail(rows, value):
        return jnp.broadcast_to(value, (rows, LANES))

    def turned(ref, f, x):
        return jnp.transpose(ref[f : f + 8, x : x + 8, :], (1, 0, 2))

    for first, last, start, count in (
        (old_first, old_last, 0, OLD),
        (new_first, new_last, OLD, NEW),
    ):
        for f in range(0, count, 8):
            for x in range(0, HALF, 8):
                at = (slice(x, x + 8), slice(start + f, start + f + 8), slice(None))
                near, far = turned(last, f, x), turned(last, f, x + HALF)
                y_top[at] = jnp.where(low_half[None], pltpu.roll(near, NZ, 2), far)
                near, far = turned(first, f, x), turned(first, f, x + HALF)
                y_low[at] = jnp.where(low_half[None], near, pltpu.roll(far, NZ, 2))
    near, far = conduct[:HALF, width - LANES :], conduct[HALF:, width - LANES :]
    top_line = jnp.where(low_half, pltpu.roll(near, NZ, 1), far)
    near, far = conduct[:HALF, :LANES], conduct[HALF:, :LANES]
    low_line = jnp.where(low_half, near, pltpu.roll(far, NZ, 1))
    for r in range(HALF):
        y_top[r, ALL:FACE, :] = tail(8, top_line[r : r + 1])
        y_low[r, ALL:FACE, :] = tail(8, low_line[r : r + 1])
    for j in range(CHUNKS):
        here = slice(j * LANES, (j + 1) * LANES)
        for out, row in ((x_top, ROWS - 1), (x_low, 0)):
            out[j, ALL : ALL + 8, :] = tail(8, conduct[row : row + 1, here])
            out[j, ALL + 8 : XFACE, :] = tail(8, drift[row : row + 1, here])

    shape = (ROWS, width)
    lane = lanes_of(shape)
    row = rows_of(shape)
    z_index = lane % NZ
    z_down, z_up = z_terms(conduct, z_index)
    half = 0.5 * conduct
    from_low_y = 0.5 * (conduct + pltpu.roll(conduct, NZ, 1))
    from_high_y = 0.5 * (conduct + pltpu.roll(conduct, width - NZ, 1))
    from_low_x = 0.5 * (conduct + pltpu.roll(conduct, 1, 0))
    from_high_x = 0.5 * (conduct + pltpu.roll(conduct, ROWS - 1, 0))
    y_down = jnp.where(lane < NZ, 0.0, from_low_y)
    y_up = jnp.where(lane >= width - NZ, 0.0, from_high_y)
    x_down = jnp.where(row == 0, 0.0, from_low_x)
    x_up = jnp.where(row == ROWS - 1, 0.0, from_high_x)
    pull = jnp.where(row == 0, 0.0, drift)
    x_last = jnp.where(position(ALONG_X) == lax.axis_size(ALONG_X) - 1, 1.0, 0.0)
    y_last = jnp.where(position(ALONG_Y) == lax.axis_size(ALONG_Y) - 1, 1.0, 0.0)
    shifts = common_shifts(conductivity, damping, drift_speed, heat_capacity)
    border = jnp.where(row == ROWS - 1, half * x_last, 0.0) + jnp.where(
        lane >= width - NZ, half * y_last, 0.0
    )
    keep_coef = coef_writer(coef)
    total = z_down + z_up + y_down + y_up + x_down + x_up + pull + loss + border
    keep_coef(0, x_down + pull)
    keep_coef(1, x_up)
    keep_coef(2, y_down)
    keep_coef(3, y_up)
    keep_coef(4, jnp.where(z_index == 0, 0.0, z_down))
    keep_coef(5, jnp.where(z_index == NZ - 1, 0.0, z_up))
    keep_coef(6, shifts[0] - total)
    keep_coef(7, capacity - shifts[1])
    for copy in copies:
        copy.wait()


def gram_kernel(
    sensor_cells, coef, old, new, source, out, sensed, rows_out, first, second, old_raw, new_raw, source_raw, rows, sources, sems, out_sems
):
    width = CHUNKS * LANES
    groups = ROWS // GROUP
    low_half = lanes_of((1, LANES)) < NZ

    def incoming(block):
        at = pl.ds(pl.multiple_of(block * 8, 8), 8)
        return [
            pltpu.make_async_copy(field.at[:, at, :], raw.at[:, at, :], sems.at[k, block])
            for k, (field, raw) in enumerate(
                ((old, old_raw), (new, new_raw), (source, source_raw))
            )
        ]

    def arrange(block):
        for copy in incoming(block):
            copy.wait()
        start = pl.multiple_of(block * 8, 8)
        turn(old_raw, rows, start, 0, OLD, 0)
        turn(new_raw, rows, start, 0, NEW, OLD)
        turn(source_raw, sources, start, 0, NEW, 0)

    def fill(stack, group):
        for r in range(GROUP):
            x = group * GROUP + r
            below = jnp.maximum(x - 1, 0)
            above = jnp.minimum(x + 1, ROWS - 1)
            mid = [rows[x, :, j * LANES : (j + 1) * LANES] for j in range(CHUNKS)]
            swapped = [pltpu.roll(value, NZ, 1) for value in mid]
            for j in range(CHUNKS):
                here = slice(j * LANES, (j + 1) * LANES)
                left = jnp.where(low_half, swapped[max(j - 1, 0)], swapped[j])
                right = jnp.where(low_half, swapped[j], swapped[min(j + 1, CHUNKS - 1)])

                def scale(index):
                    return coef[index * CHUNKS + j, pl.ds(x, 1), :]

                value = mid[j]
                moved = (
                    scale(0) * rows[below, :, here]
                    + scale(1) * rows[above, :, here]
                    + scale(2) * left
                    + scale(3) * right
                    + scale(4) * pltpu.roll(value, 1, 1)
                    + scale(5) * pltpu.roll(value, LANES - 1, 1)
                    + scale(6) * value
                )
                at = pl.ds((r * CHUNKS + j) * LANES, LANES)
                high, low = split(value, 2)
                stack[0:ALL, at] = high
                stack[LANES : LANES + ALL, at] = low
                high, low = split(sources[x, :, here], 2)
                stack[ALL:LANES, at] = high
                stack[LANES + ALL : 2 * LANES, at] = low
                base = 2 * LANES
                for item in (moved, scale(7) * value):
                    high, low = split(item, 2)
                    stack[base : base + ALL, at] = high
                    stack[base + ALL : base + 2 * ALL, at] = low
                    base += 2 * ALL

    def add(stack):
        out[...] += lax.dot_general(
            stack[...],
            stack[0 : 2 * LANES, :],
            (((1,), (1,)), ((), ())),
            preferred_element_type=F32,
        )

    for block in range(ROWS // 8):
        for copy in incoming(block):
            copy.start()
    out[...] = jnp.zeros(out.shape, F32)
    arrange(0)
    fill(first, 0)

    def step(i, carry):
        arrange(i + 1)
        add(first)
        fill(second, 2 * i + 1)
        add(second)
        fill(first, 2 * i + 2)
        return carry

    lax.fori_loop(0, groups // 2 - 1, step, 0)
    outgoing = [
        pltpu.make_async_copy(rows.at[pl.ds(x, 8)], rows_out.at[pl.ds(x, 8)], out_sems.at[x // 8])
        for x in range(0, ROWS, 8)
    ]
    for copy in outgoing:
        copy.start()
    add(first)
    fill(second, groups - 1)
    add(second)

    lane = lanes_of((ALL, LANES))
    sensed[...] = jnp.zeros(sensed.shape, F32)
    row_span = width * lax.axis_size(ALONG_Y)
    index_x, index_y = position(ALONG_X), position(ALONG_Y)

    def sense(p, carry):
        cell = sensor_cells[p]
        x_global = cell // row_span
        remainder = cell % row_span
        inside = (x_global // ROWS == index_x) & (remainder // width == index_y)

        @pl.when(inside)
        def _():
            x = x_global % ROWS
            column = remainder % width
            found = jnp.zeros((ALL, LANES), F32)
            for j in range(CHUNKS):
                value = rows[x, :, j * LANES : (j + 1) * LANES]
                found = jnp.where(lane == column - j * LANES, value, found)
            picked = jnp.sum(found, axis=1, keepdims=True)
            sensed[...] = jnp.where(lane == p, picked, sensed[...])

        return carry

    lax.fori_loop(0, sensor_cells.shape[0], sense, 0)
    for copy in outgoing:
        copy.wait()


def fold(block, rows):
    return (
        block[0:rows, 0:LANES]
        + block[rows : 2 * rows, 0:LANES]
        + (block[0:rows, LANES:] + block[rows : 2 * rows, LANES:])
    )


def face_kernel(gram, sensed, y_own, y_near, x_own, x_near, out, diffs, scaled):
    tiles = HALF + CHUNKS
    zero_rows = jnp.zeros((LANES - ALL, tiles * LANES), BF16)
    scaled[ALL:LANES, :] = zero_rows
    scaled[LANES + ALL : 2 * LANES, :] = zero_rows
    for t in range(tiles):
        at = pl.ds(t * LANES, LANES)
        if t < HALF:
            own, near = y_own.at[t], y_near.at[t]
        else:
            own, near = x_own.at[t - HALF], x_near.at[t - HALF]
        value = own[0:ALL, :]
        diff = value - near[0:ALL, :]
        edge = 0.5 * (own[ALL : ALL + 1, :] + near[ALL : ALL + 1, :])
        weighted = edge * diff
        if t >= HALF:
            weighted = weighted + own[ALL + 8 : ALL + 9, :] * value
        high, low = split(diff, 2)
        diffs[0:ALL, at] = high
        diffs[ALL : 2 * ALL, at] = low
        high, low = split(weighted, 2)
        scaled[0:ALL, at] = high
        scaled[LANES : LANES + ALL, at] = low
    faces = lax.dot_general(
        diffs[...], scaled[...], (((1,), (1,)), ((), ())), preferred_element_type=F32
    )
    crossed = fold(gram[0 : 2 * LANES, :], LANES)
    overlap = crossed[0:ALL]
    source = crossed[ALL:LANES]
    base = 2 * LANES
    moved = fold(gram[base : base + 2 * ALL, :], ALL) - fold(faces, ALL)
    base += 2 * ALL
    massed = fold(gram[base : base + 2 * ALL, :], ALL)
    source = jnp.concatenate([source, jnp.zeros((LANES - NEW, LANES), F32)], axis=0).T
    source = pltpu.roll(source[0:ALL, :], ALL, 1)
    lane = lanes_of((ALL, LANES))
    row = rows_of((ALL, LANES))
    diagonal = jnp.sum(jnp.where(lane == row, massed, 0.0), axis=1, keepdims=True)
    upper = jnp.where(row >= lane, overlap, massed)
    out[0:ALL, :] = jnp.where(lane < ALL, upper, source)
    extra = jnp.where(lane == ALL + 16, diagonal, pltpu.roll(sensed[...], ALL, 1))
    out[ALL : 2 * ALL, :] = jnp.where(lane < ALL, moved, extra)
    out[2 * ALL : PAYLOAD, :] = jnp.zeros((PAYLOAD - 2 * ALL, LANES), F32)


def small_dot(left, right):
    return lax.dot_general(
        left, right, (((1,), (0,)), ((), ())), preferred_element_type=F32, precision=HIGH
    )


def flip(block):
    rows, columns = block.shape
    if rows < LANES:
        block = jnp.concatenate([block, jnp.zeros((LANES - rows, columns), F32)], axis=0)
    if columns < LANES:
        block = jnp.concatenate([block, jnp.zeros((LANES, LANES - columns), F32)], axis=1)
    return block.T[0:columns, 0:rows]


def lower_inverse(gram):
    shape = (NEW, LANES)
    lane, row = lanes_of(shape), rows_of(shape)
    work = jnp.concatenate(
        [gram, jnp.zeros((NEW, LANES - NEW), F32)], axis=1
    ) + jnp.where(lane == row + NEW, 1.0, 0.0)
    for k in range(NEW):
        pivot = work[k : k + 1, k : k + 1]
        line = work[k : k + 1, :] / pivot
        factor = jnp.where(row[:, 0:1] > k, work[:, k : k + 1], 0.0)
        work = work - factor * line
    pivots = jnp.sum(jnp.where(lane == row, work, 0.0), axis=1, keepdims=True)
    return (work / jnp.sqrt(pivots))[:, NEW : 2 * NEW]


def basis_kernel(
    volume,
    region_ref,
    conductivity,
    damping,
    drift_speed,
    heat_capacity,
    summed,
    y_before,
    y_after,
    x_before,
    x_after,
    rows_in,
    basis_out,
    applied_out,
    stiff_block,
    stiff_row,
    capacity_block,
    sensor_block,
    source_block,
    rows,
    coef,
    field,
    applied,
    basis_raw,
    applied_raw,
    low_y,
    high_y,
    first,
    second,
    weights,
    sems,
    basis_sems,
    applied_sems,
):
    width = CHUNKS * LANES

    incoming = [
        pltpu.make_async_copy(rows_in.at[pl.ds(x, 8)], rows.at[pl.ds(x, 8)], sems.at[x // 8])
        for x in range(0, ROWS, 8)
    ]
    for copy in incoming:
        copy.start()
    shifts = common_shifts(conductivity, damping, drift_speed, heat_capacity)

    lane = lanes_of((ALL, LANES))
    row = rows_of((ALL, LANES))
    top = summed[0:ALL, :] * volume
    bottom = summed[ALL : 2 * ALL, :] * volume
    upper = jnp.where(lane < ALL, top, 0.0)
    low_part = jnp.where(lane <= row, upper, 0.0)
    high_part = jnp.where(lane > row, upper, 0.0)
    diagonal = jnp.where(lane == row, low_part, 0.0)
    overlap = (low_part - diagonal)[:, 0:ALL] + flip(low_part[:, 0:ALL])
    mass_diagonal = jnp.where(lane == row, bottom[:, ALL + 16 : ALL + 17], 0.0)
    massed = (high_part + mass_diagonal)[:, 0:ALL] + flip(high_part[:, 0:ALL])
    moved = flip(bottom[:, 0:ALL])
    source = top[:, ALL:LANES]
    sensed = summed[ALL : 2 * ALL, ALL : ALL + 16]

    old_gram = overlap[0:OLD, 0:OLD]
    first_weights = overlap[0:OLD, OLD:ALL]
    new_gram = overlap[OLD:ALL, OLD:ALL]
    second_weights = first_weights - small_dot(old_gram, first_weights)
    left_over = second_weights - small_dot(old_gram, second_weights)
    both = first_weights + second_weights
    both_t = flip(both)
    gram = new_gram - small_dot(flip(first_weights), both) - small_dot(both_t, left_over)
    inverse = lower_inverse(gram)
    mix = jnp.concatenate([-small_dot(inverse, both_t), inverse], axis=1)
    mix_t = flip(mix)
    mix_wide = jnp.concatenate([mix, jnp.zeros((NEW, LANES - ALL), F32)], axis=1)
    for k, piece in enumerate(split(mix_wide, 3)):
        for s in range(PARTS):
            weights[k * NEW : (k + 1) * NEW, s * LANES : (s + 1) * LANES] = piece

    conduct, drift, loss, capacity = cell_fields(
        region_ref, conductivity, damping, drift_speed, heat_capacity
    )
    shape = (ROWS, width)
    lane = lanes_of(shape)
    row = rows_of(shape)
    z_index = lane % NZ
    z_down, z_up = z_terms(conduct, z_index)
    low_half = lanes_of((1, LANES)) < NZ

    def face_conduct(ref, at_low):
        tile = jnp.concatenate([ref[r, ALL : ALL + 1, :] for r in range(HALF)], axis=0)
        turned = pltpu.roll(tile, NZ, 1)
        pair = [tile, turned] if at_low else [turned, tile]
        return jnp.concatenate(pair, axis=0)

    blank = jnp.zeros((ROWS, width - LANES), F32)
    before = jnp.concatenate([face_conduct(y_before, True), blank], axis=1)
    after = jnp.concatenate([blank, face_conduct(y_after, False)], axis=1)
    near_y = jnp.where(lane < NZ, before, pltpu.roll(conduct, NZ, 1))
    far_y = jnp.where(lane >= width - NZ, after, pltpu.roll(conduct, width - NZ, 1))
    x_line = [
        jnp.concatenate([ref[j, ALL : ALL + 1, :] for j in range(CHUNKS)], axis=1)
        for ref in (x_before, x_after)
    ]
    near_x = jnp.where(row == 0, x_line[0], pltpu.roll(conduct, 1, 0))
    far_x = jnp.where(row == ROWS - 1, x_line[1], pltpu.roll(conduct, ROWS - 1, 0))
    keep_coef = coef_writer(coef)
    y_down, y_up = 0.5 * (conduct + near_y), 0.5 * (conduct + far_y)
    x_down, x_up = 0.5 * (conduct + near_x), 0.5 * (conduct + far_x)
    keep_coef(0, x_down + drift)
    keep_coef(1, x_up)
    keep_coef(2, y_down)
    keep_coef(3, y_up)
    keep_coef(4, jnp.where(z_index == 0, 0.0, z_down))
    keep_coef(5, jnp.where(z_index == NZ - 1, 0.0, z_up))
    keep_coef(6, -(z_down + z_up + y_down + y_up + x_down + x_up + drift + loss))

    zero_rows = jnp.zeros((LANES - ALL, width), BF16)
    for stack in (first, second):
        for s in range(PARTS):
            stack[s * LANES + ALL : (s + 1) * LANES, :] = zero_rows

    def fill(stack, tiles):
        for j, tile in enumerate(tiles):
            for s, piece in enumerate(split(tile, PARTS)):
                stack[s * LANES : s * LANES + ALL, pl.ds(j * LANES, LANES)] = piece

    def product(stack):
        result = jnp.dot(weights[...], stack[...], preferred_element_type=F32)
        return result[0:NEW] + (result[NEW : 2 * NEW] + result[2 * NEW : 3 * NEW])

    for ref, place in ((x_before, 0), (x_after, ROWS + 1)):
        fill(first, [ref[j, 0:ALL, :] for j in range(CHUNKS)])
        field[place] = product(first)
    for ref, target, at_low in ((y_before, low_y, True), (y_after, high_y, False)):
        for g in range(HALF // CHUNKS):
            stack = first if g % 2 == 0 else second
            fill(stack, [ref[g * CHUNKS + j, 0:ALL, :] for j in range(CHUNKS)])
            value = product(stack)
            for j in range(CHUNKS):
                tile = value[:, j * LANES : (j + 1) * LANES]
                turned = pltpu.roll(tile, NZ, 1)
                r = g * CHUNKS + j
                target[r] = tile if at_low else turned
                target[r + HALF] = turned if at_low else tile

    def load(stack, x):
        fill(stack, [rows[x, :, j * LANES : (j + 1) * LANES] for j in range(CHUNKS)])

    def outgoing(block):
        at = pl.ds(pl.multiple_of(block * 8, 8), 8)
        return [
            pltpu.make_async_copy(basis_raw.at[:, at, :], basis_out.at[:, at, :], basis_sems.at[block]),
            pltpu.make_async_copy(
                applied_raw.at[:, at, :], applied_out.at[:, at, :], applied_sems.at[block]
            ),
        ]

    def flush(block):
        start = pl.multiple_of(block * 8, 8)
        turn_back(field, basis_raw, start, 1, NEW)
        turn_back(applied, applied_raw, start, 0, NEW)
        for copy in outgoing(block):
            copy.start()

    def keep(x, stack):
        field[x + 1] = product(stack)

    def apply(x):
        mid = [field[x + 1, :, j * LANES : (j + 1) * LANES] for j in range(CHUNKS)]
        swapped = [pltpu.roll(value, NZ, 1) for value in mid]
        for j in range(CHUNKS):
            here = slice(j * LANES, (j + 1) * LANES)
            before_j = swapped[j - 1] if j > 0 else low_y[x]
            after_j = swapped[j + 1] if j < CHUNKS - 1 else high_y[x]
            left = jnp.where(low_half, before_j, swapped[j])
            right = jnp.where(low_half, swapped[j], after_j)

            def scale(index):
                return coef[index * CHUNKS + j, pl.ds(x, 1), :]

            value = mid[j]
            applied[x, :, here] = (
                scale(0) * field[x, :, here]
                + scale(1) * field[x + 2, :, here]
                + scale(2) * left
                + scale(3) * right
                + scale(4) * pltpu.roll(value, 1, 1)
                + scale(5) * pltpu.roll(value, LANES - 1, 1)
                + scale(6) * value
            )

    for copy in incoming:
        copy.wait()
    load(first, 0)
    load(second, 1)
    keep(0, first)

    def step(i, carry):
        x = 2 * i + 1
        keep(x, second)
        load(first, x + 1)
        apply(x - 1)
        keep(x + 1, first)
        load(second, x + 2)
        apply(x)
        pl.when((i + 1) % 4 == 0)(lambda: flush((i + 1) // 4 - 1))
        return carry

    lax.fori_loop(0, ROWS // 2 - 1, step, 0)
    keep(ROWS - 1, second)
    apply(ROWS - 2)
    apply(ROWS - 1)
    flush(ROWS // 8 - 1)

    outside = small_dot(left_over, flip(inverse))
    unit = jnp.where(
        lanes_of((NEW, NEW)) == rows_of((NEW, NEW)), 1.0, 0.0
    )
    columns = small_dot(moved, mix_t)
    stiff_columns = columns[0:OLD] - shifts[0] * outside
    stiff_rest = small_dot(mix, columns) - shifts[0] * unit
    stiff_block[...] = flip(jnp.concatenate([stiff_columns, stiff_rest], axis=0))
    stiff_row[...] = small_dot(mix, moved[:, 0:OLD]) - shifts[0] * flip(outside)
    columns = small_dot(massed, mix_t)
    mass_columns = columns[0:OLD] + shifts[1] * outside
    mass_rest = small_dot(mix, columns) + shifts[1] * unit
    capacity_block[...] = flip(jnp.concatenate([mass_columns, mass_rest], axis=0))
    sensor_block[...] = flip(small_dot(mix, sensed))
    source_block[...] = small_dot(mix, source)

    for block in range(ROWS // 8):
        for copy in outgoing(block):
            copy.wait()


def swap(pieces, axes):
    return lax.all_to_all(pieces, axes, 0, 0)


def spread(block, axes):
    count = lax.axis_size(axes)
    return jnp.sum(swap(block.reshape(count, -1, LANES), axes), axis=0)


def copies_of(piece, axes):
    return swap(jnp.broadcast_to(piece[None], (lax.axis_size(axes), *piece.shape)), axes)


def gathered(piece, axes):
    return copies_of(piece, axes).reshape(-1, LANES)


def all_sum(block):
    inner, outer = ("core", "z"), ("x", "y")
    piece = spread(block, inner)
    piece = jnp.sum(copies_of(piece, outer), axis=0)
    return gathered(piece, inner)


def per_device(
    old_basis,
    new_block,
    source_matrix,
    region_map,
    conductivity,
    damping,
    drift_speed,
    heat_capacity,
    sensor_cells,
):
    width_x = old_basis.shape[1]
    width_yz = old_basis.shape[2]
    count_x = lax.axis_size(ALONG_X)
    count_y = lax.axis_size(ALONG_Y)
    volume = 1.0 / (width_x * count_x * width_yz * count_y)
    whole = pl.BlockSpec(memory_space=pltpu.VMEM)
    scalar = pl.BlockSpec(memory_space=pltpu.SMEM)
    hbm = pl.BlockSpec(memory_space=pl.ANY)
    params = pltpu.CompilerParams(vmem_limit_bytes=VMEM_LIMIT)

    def shape(*sizes):
        return jax.ShapeDtypeStruct(sizes, F32)

    def column(count, j):
        return pl.BlockSpec((count, ROWS, LANES), lambda *_: (0, 0, j))

    tables = (conductivity, damping, drift_speed, heat_capacity)

    y_top, y_low, x_top, x_low, coef = pl.pallas_call(
        pack_kernel,
        grid=(1,),
        out_shape=[
            shape(HALF, FACE, LANES),
            shape(HALF, FACE, LANES),
            shape(CHUNKS, XFACE, LANES),
            shape(CHUNKS, XFACE, LANES),
            shape(8 * CHUNKS, ROWS, LANES),
        ],
        in_specs=[whole]
        + [scalar] * 4
        + [hbm] * 2
        + [column(OLD, 0), column(OLD, CHUNKS - 1), column(NEW, 0), column(NEW, CHUNKS - 1)],
        out_specs=[whole] * 5,
        scratch_shapes=[pltpu.SemaphoreType.DMA((4 * CHUNKS,))],
        compiler_params=params,
        name="pack",
    )(
        region_map,
        *tables,
        old_basis,
        new_block,
        old_basis,
        old_basis,
        new_block,
        new_block,
    )

    def onward(value, axis):
        return lax.ppermute(value, axis, [(i, i + 1) for i in range(lax.axis_size(axis) - 1)])

    def backward(value, axis):
        return lax.ppermute(value, axis, [(i + 1, i) for i in range(lax.axis_size(axis) - 1)])

    y_before = onward(y_top, ALONG_Y)
    x_before = onward(x_top, ALONG_X)
    y_after = backward(y_low, ALONG_Y)
    x_after = backward(x_low, ALONG_X)

    stack_rows = 2 * LANES + 4 * ALL
    stack_width = GROUP * CHUNKS * LANES
    gram, sensed, rows = pl.pallas_call(
        gram_kernel,
        out_shape=[
            shape(stack_rows, 2 * LANES),
            shape(ALL, LANES),
            shape(ROWS, ALL, width_yz),
        ],
        in_specs=[scalar, whole] + [hbm] * 3,
        out_specs=[whole, whole, hbm],
        scratch_shapes=[
            pltpu.VMEM((stack_rows, stack_width), BF16),
            pltpu.VMEM((stack_rows, stack_width), BF16),
            pltpu.VMEM(old_basis.shape, F32),
            pltpu.VMEM(new_block.shape, F32),
            pltpu.VMEM(source_matrix.shape, F32),
            pltpu.VMEM((ROWS, ALL, width_yz), F32),
            pltpu.VMEM((ROWS, NEW, width_yz), F32),
            pltpu.SemaphoreType.DMA((3, 4)),
            pltpu.SemaphoreType.DMA((4,)),
        ],
        compiler_params=params,
        cost_estimate=pl.CostEstimate(
            flops=2 * stack_rows * 2 * LANES * width_x * width_yz,
            bytes_accessed=(ALL + NEW) * 4 * width_x * width_yz,
            transcendentals=0,
        ),
        name="gram",
    )(sensor_cells, coef, old_basis, new_block, source_matrix)
    y_before, y_after, x_before, x_after, gram = lax.optimization_barrier(
        (y_before, y_after, x_before, x_after, gram)
    )

    face_width = (HALF + CHUNKS) * LANES
    partial = pl.pallas_call(
        face_kernel,
        out_shape=shape(PAYLOAD, LANES),
        in_specs=[whole] * 6,
        out_specs=whole,
        scratch_shapes=[
            pltpu.VMEM((2 * ALL, face_width), BF16),
            pltpu.VMEM((2 * LANES, face_width), BF16),
        ],
        compiler_params=params,
        name="faces",
    )(gram, sensed, y_low, y_before, x_low, x_before)

    summed = all_sum(partial)

    results = pl.pallas_call(
        functools.partial(basis_kernel, volume),
        out_shape=[
            shape(*new_block.shape),
            shape(*new_block.shape),
            shape(NEW, ALL),
            shape(NEW, OLD),
            shape(NEW, ALL),
            shape(16, NEW),
            shape(NEW, NEW),
        ],
        in_specs=[whole] + [scalar] * 4 + [whole] * 5 + [hbm],
        out_specs=[hbm, hbm] + [whole] * 5,
        scratch_shapes=[
            pltpu.VMEM((ROWS, ALL, width_yz), F32),
            pltpu.VMEM((7 * CHUNKS, ROWS, LANES), F32),
            pltpu.VMEM((ROWS + 2, NEW, width_yz), F32),
            pltpu.VMEM((ROWS, NEW, width_yz), F32),
            pltpu.VMEM(new_block.shape, F32),
            pltpu.VMEM(new_block.shape, F32),
            pltpu.VMEM((ROWS, NEW, LANES), F32),
            pltpu.VMEM((ROWS, NEW, LANES), F32),
            pltpu.VMEM((PARTS * LANES, width_yz), BF16),
            pltpu.VMEM((PARTS * LANES, width_yz), BF16),
            pltpu.VMEM((3 * NEW, PARTS * LANES), BF16),
            pltpu.SemaphoreType.DMA((4,)),
            pltpu.SemaphoreType.DMA((4,)),
            pltpu.SemaphoreType.DMA((4,)),
        ],
        compiler_params=params,
        name="basis",
    )(
        region_map,
        *tables,
        summed,
        y_before,
        y_after,
        x_before,
        x_after,
        rows,
    )
    basis, applied, stiff_block, stiff_row, capacity_block, sensor_block, source_block = results
    return (
        basis,
        applied,
        stiff_block.T,
        stiff_row,
        capacity_block.T,
        sensor_block,
        source_block,
    )


def solution(mesh):
    mesh = jax.sharding.Mesh(mesh.devices.reshape(4, 2, 8, 4), ALONG_X + ALONG_Y)
    fields = P(None, ALONG_X, ALONG_Y)
    in_specs = (fields, fields, fields, P(ALONG_X, ALONG_Y), P(), P(), P(), P(), P())
    out_specs = (fields, fields, P(), P(), P(), P(), P())
    return jax.shard_map(
        per_device, mesh=mesh, in_specs=in_specs, out_specs=out_specs, check_vma=False
    )
```

```python
import functools

import jax
import jax.numpy as jnp
from jax import lax
from jax.experimental import pallas as pl
from jax.experimental.pallas import tpu as pltpu
from jax.sharding import PartitionSpec as P

NZ = 64
LANES = 128
OLD = 64
NEW = 32
ALL = OLD + NEW
ROWS = 32
CHUNKS = 4
HALF = ROWS // 2
GROUP = 4
PARTS = 3
FACE = ALL + 8
XFACE = ALL + 16
PAYLOAD = 2 * LANES
ALONG_X = ("x", "core")
ALONG_Y = ("z", "y")
F32 = jnp.float32
BF16 = jnp.bfloat16
HIGH = lax.Precision.HIGHEST
VMEM_LIMIT = 56 * 1024 * 1024


def position(axes):
    slow, fast = axes
    return lax.axis_index(slow) * lax.axis_size(fast) + lax.axis_index(fast)


def odd_lanes(axes):
    return jnp.broadcast_to(position(axes) % 2, (1, LANES)) == 1


def split(value, count):
    pieces = []
    for _ in range(count):
        piece = value.astype(BF16)
        pieces.append(piece)
        value = value - piece.astype(F32)
    return pieces


def lanes_of(shape):
    return lax.broadcasted_iota(jnp.int32, shape, len(shape) - 1)


def rows_of(shape):
    return lax.broadcasted_iota(jnp.int32, shape, 0)


def table_mean(table):
    total = table[0]
    for r in range(1, 8):
        total = total + table[r]
    return total * 0.125


def common_shifts(conductivity, damping, drift_speed, heat_capacity):
    loss = damping[0] * heat_capacity[0]
    for r in range(1, 8):
        loss = loss + damping[r] * heat_capacity[r]
    stiff = 6.0 * table_mean(conductivity) + table_mean(drift_speed) + loss * 0.125
    return stiff, table_mean(heat_capacity)


def turn(source, target, start, shift, fields, base):
    for f in range(0, fields, 8):
        for j in range(CHUNKS):
            here = slice(j * LANES, (j + 1) * LANES)
            tile = source[f : f + 8, pl.ds(start, 8), here]
            target[pl.ds(start + shift, 8), base + f : base + f + 8, here] = jnp.transpose(
                tile, (1, 0, 2)
            )


def turn_back(source, target, start, shift, fields):
    for f in range(0, fields, 8):
        for j in range(CHUNKS):
            here = slice(j * LANES, (j + 1) * LANES)
            tile = source[pl.ds(start + shift, 8), f : f + 8, here]
            target[f : f + 8, pl.ds(start, 8), here] = jnp.transpose(tile, (1, 0, 2))


def cell_fields(region_ref, conductivity, damping, drift_speed, heat_capacity):
    region = region_ref[...]
    conduct = jnp.zeros(region.shape, F32)
    drift = jnp.zeros(region.shape, F32)
    loss = jnp.zeros(region.shape, F32)
    capacity = jnp.zeros(region.shape, F32)
    for r in range(8):
        here = region == r
        conduct = jnp.where(here, conductivity[r], conduct)
        drift = jnp.where(here, drift_speed[r], drift)
        loss = jnp.where(here, damping[r] * heat_capacity[r], loss)
        capacity = jnp.where(here, heat_capacity[r], capacity)
    return conduct, drift, loss, capacity


def z_terms(conduct, z_index):
    low_z = jnp.where(z_index == 0, 0.0, pltpu.roll(conduct, 1, 1))
    high_z = jnp.where(z_index == NZ - 1, 0.0, pltpu.roll(conduct, conduct.shape[1] - 1, 1))
    return 0.5 * (conduct + low_z), 0.5 * (conduct + high_z)


def coef_writer(coef):
    def keep_coef(index, value):
        for j in range(CHUNKS):
            coef[index * CHUNKS + j] = value[:, j * LANES : (j + 1) * LANES]

    return keep_coef


def pack_kernel(
    region_ref,
    conductivity,
    damping,
    drift_speed,
    heat_capacity,
    old,
    new,
    old_first,
    old_last,
    new_first,
    new_last,
    y_first,
    y_second,
    x_first,
    x_second,
    coef,
    sems,
):
    width = CHUNKS * LANES
    copies = []
    odd_x, odd_y = odd_lanes(ALONG_X), odd_lanes(ALONG_Y)
    parity = position(ALONG_X) % 2
    for out, row, base in (
        (x_first, (1 - parity) * (ROWS - 1), 0),
        (x_second, parity * (ROWS - 1), 2 * CHUNKS),
    ):
        for j in range(CHUNKS):
            here = pl.ds(j * LANES, LANES)
            for field, start, count, shift in ((old, 0, OLD, 0), (new, OLD, NEW, CHUNKS)):
                copies.append(
                    pltpu.make_async_copy(
                        field.at[:, row, here],
                        out.at[j, pl.ds(start, count), :],
                        sems.at[base + shift + j],
                    )
                )
    for copy in copies:
        copy.start()
    conduct, drift, loss, capacity = cell_fields(
        region_ref, conductivity, damping, drift_speed, heat_capacity
    )
    low_half = lanes_of((1, LANES)) < NZ

    def tail(rows, value):
        return jnp.broadcast_to(value, (rows, LANES))

    def turned(ref, f, x):
        return jnp.transpose(ref[f : f + 8, x : x + 8, :], (1, 0, 2))

    for first, last, start, count in (
        (old_first, old_last, 0, OLD),
        (new_first, new_last, OLD, NEW),
    ):
        for f in range(0, count, 8):
            for x in range(0, HALF, 8):
                at = (slice(x, x + 8), slice(start + f, start + f + 8), slice(None))
                near, far = turned(last, f, x), turned(last, f, x + HALF)
                top = jnp.where(low_half[None], pltpu.roll(near, NZ, 2), far)
                near, far = turned(first, f, x), turned(first, f, x + HALF)
                low = jnp.where(low_half[None], near, pltpu.roll(far, NZ, 2))
                y_first[at] = jnp.where(odd_y[None], low, top)
                y_second[at] = jnp.where(odd_y[None], top, low)
    near, far = conduct[:HALF, width - LANES :], conduct[HALF:, width - LANES :]
    top_line = jnp.where(low_half, pltpu.roll(near, NZ, 1), far)
    near, far = conduct[:HALF, :LANES], conduct[HALF:, :LANES]
    low_line = jnp.where(low_half, near, pltpu.roll(far, NZ, 1))
    first_line = jnp.where(odd_y, low_line, top_line)
    second_line = jnp.where(odd_y, top_line, low_line)
    for r in range(HALF):
        y_first[r, ALL:FACE, :] = tail(8, first_line[r : r + 1])
        y_second[r, ALL:FACE, :] = tail(8, second_line[r : r + 1])
    for j in range(CHUNKS):
        here = slice(j * LANES, (j + 1) * LANES)
        for k, value in enumerate((conduct, drift)):
            at = slice(ALL + 8 * k, ALL + 8 * k + 8)
            top, low = value[ROWS - 1 : ROWS, here], value[0:1, here]
            x_first[j, at, :] = tail(8, jnp.where(odd_x, low, top))
            x_second[j, at, :] = tail(8, jnp.where(odd_x, top, low))

    shape = (ROWS, width)
    lane = lanes_of(shape)
    row = rows_of(shape)
    z_index = lane % NZ
    z_down, z_up = z_terms(conduct, z_index)
    half = 0.5 * conduct
    from_low_y = 0.5 * (conduct + pltpu.roll(conduct, NZ, 1))
    from_high_y = 0.5 * (conduct + pltpu.roll(conduct, width - NZ, 1))
    from_low_x = 0.5 * (conduct + pltpu.roll(conduct, 1, 0))
    from_high_x = 0.5 * (conduct + pltpu.roll(conduct, ROWS - 1, 0))
    y_down = jnp.where(lane < NZ, 0.0, from_low_y)
    y_up = jnp.where(lane >= width - NZ, 0.0, from_high_y)
    x_down = jnp.where(row == 0, 0.0, from_low_x)
    x_up = jnp.where(row == ROWS - 1, 0.0, from_high_x)
    pull = jnp.where(row == 0, 0.0, drift)
    x_last = jnp.where(position(ALONG_X) == lax.axis_size(ALONG_X) - 1, 1.0, 0.0)
    y_last = jnp.where(position(ALONG_Y) == lax.axis_size(ALONG_Y) - 1, 1.0, 0.0)
    shifts = common_shifts(conductivity, damping, drift_speed, heat_capacity)
    border = jnp.where(row == ROWS - 1, half * x_last, 0.0) + jnp.where(
        lane >= width - NZ, half * y_last, 0.0
    )
    keep_coef = coef_writer(coef)
    total = z_down + z_up + y_down + y_up + x_down + x_up + pull + loss + border
    keep_coef(0, x_down + pull)
    keep_coef(1, x_up)
    keep_coef(2, y_down)
    keep_coef(3, y_up)
    keep_coef(4, jnp.where(z_index == 0, 0.0, z_down))
    keep_coef(5, jnp.where(z_index == NZ - 1, 0.0, z_up))
    keep_coef(6, shifts[0] - total)
    keep_coef(7, capacity - shifts[1])
    for copy in copies:
        copy.wait()


def gram_kernel(
    sensor_cells, coef, old, new, source, out, sensed, rows_out, first, second, old_raw, new_raw, source_raw, rows, sources, sems, out_sems
):
    width = CHUNKS * LANES
    groups = ROWS // GROUP
    low_half = lanes_of((1, LANES)) < NZ

    def incoming(block):
        at = pl.ds(pl.multiple_of(block * 8, 8), 8)
        return [
            pltpu.make_async_copy(field.at[:, at, :], raw.at[:, at, :], sems.at[k, block])
            for k, (field, raw) in enumerate(
                ((old, old_raw), (new, new_raw), (source, source_raw))
            )
        ]

    def arrange(block):
        for copy in incoming(block):
            copy.wait()
        start = pl.multiple_of(block * 8, 8)
        turn(old_raw, rows, start, 0, OLD, 0)
        turn(new_raw, rows, start, 0, NEW, OLD)
        turn(source_raw, sources, start, 0, NEW, 0)

    def fill(stack, group):
        for r in range(GROUP):
            x = group * GROUP + r
            below = jnp.maximum(x - 1, 0)
            above = jnp.minimum(x + 1, ROWS - 1)
            mid = [rows[x, :, j * LANES : (j + 1) * LANES] for j in range(CHUNKS)]
            swapped = [pltpu.roll(value, NZ, 1) for value in mid]
            for j in range(CHUNKS):
                here = slice(j * LANES, (j + 1) * LANES)
                left = jnp.where(low_half, swapped[max(j - 1, 0)], swapped[j])
                right = jnp.where(low_half, swapped[j], swapped[min(j + 1, CHUNKS - 1)])

                def scale(index):
                    return coef[index * CHUNKS + j, pl.ds(x, 1), :]

                value = mid[j]
                moved = (
                    scale(0) * rows[below, :, here]
                    + scale(1) * rows[above, :, here]
                    + scale(2) * left
                    + scale(3) * right
                    + scale(4) * pltpu.roll(value, 1, 1)
                    + scale(5) * pltpu.roll(value, LANES - 1, 1)
                    + scale(6) * value
                )
                at = pl.ds((r * CHUNKS + j) * LANES, LANES)
                high, low = split(value, 2)
                stack[0:ALL, at] = high
                stack[LANES : LANES + ALL, at] = low
                high, low = split(sources[x, :, here], 2)
                stack[ALL:LANES, at] = high
                stack[LANES + ALL : 2 * LANES, at] = low
                base = 2 * LANES
                for item in (moved, scale(7) * value):
                    high, low = split(item, 2)
                    stack[base : base + ALL, at] = high
                    stack[base + ALL : base + 2 * ALL, at] = low
                    base += 2 * ALL

    def add(stack):
        out[...] += lax.dot_general(
            stack[...],
            stack[0 : 2 * LANES, :],
            (((1,), (1,)), ((), ())),
            preferred_element_type=F32,
        )

    for block in range(ROWS // 8):
        for copy in incoming(block):
            copy.start()
    out[...] = jnp.zeros(out.shape, F32)
    arrange(0)
    fill(first, 0)

    def step(i, carry):
        arrange(i + 1)
        add(first)
        fill(second, 2 * i + 1)
        add(second)
        fill(first, 2 * i + 2)
        return carry

    lax.fori_loop(0, groups // 2 - 1, step, 0)
    outgoing = [
        pltpu.make_async_copy(rows.at[pl.ds(x, 8)], rows_out.at[pl.ds(x, 8)], out_sems.at[x // 8])
        for x in range(0, ROWS, 8)
    ]
    for copy in outgoing:
        copy.start()
    add(first)
    fill(second, groups - 1)
    add(second)

    lane = lanes_of((ALL, LANES))
    sensed[...] = jnp.zeros(sensed.shape, F32)
    row_span = width * lax.axis_size(ALONG_Y)
    index_x, index_y = position(ALONG_X), position(ALONG_Y)

    def sense(p, carry):
        cell = sensor_cells[p]
        x_global = cell // row_span
        remainder = cell % row_span
        inside = (x_global // ROWS == index_x) & (remainder // width == index_y)

        @pl.when(inside)
        def _():
            x = x_global % ROWS
            column = remainder % width
            found = jnp.zeros((ALL, LANES), F32)
            for j in range(CHUNKS):
                value = rows[x, :, j * LANES : (j + 1) * LANES]
                found = jnp.where(lane == column - j * LANES, value, found)
            picked = jnp.sum(found, axis=1, keepdims=True)
            sensed[...] = jnp.where(lane == p, picked, sensed[...])

        return carry

    lax.fori_loop(0, sensor_cells.shape[0], sense, 0)
    for copy in outgoing:
        copy.wait()


def fold(block, rows):
    return (
        block[0:rows, 0:LANES]
        + block[rows : 2 * rows, 0:LANES]
        + (block[0:rows, LANES:] + block[rows : 2 * rows, LANES:])
    )


def face_kernel(
    gram,
    sensed,
    y_first,
    y_second,
    x_first,
    x_second,
    y_from_first,
    y_from_second,
    x_from_first,
    x_from_second,
    out,
    diffs,
    scaled,
):
    odd_x, odd_y = odd_lanes(ALONG_X), odd_lanes(ALONG_Y)
    tiles = HALF + CHUNKS
    zero_rows = jnp.zeros((LANES - ALL, tiles * LANES), BF16)
    scaled[ALL:LANES, :] = zero_rows
    scaled[LANES + ALL : 2 * LANES, :] = zero_rows
    for t in range(tiles):
        at = pl.ds(t * LANES, LANES)
        if t < HALF:
            own = jnp.where(odd_y, y_first[t], y_second[t])
            near = jnp.where(odd_y, y_from_first[t], y_from_second[t])
        else:
            own = jnp.where(odd_x, x_first[t - HALF], x_second[t - HALF])
            near = jnp.where(odd_x, x_from_first[t - HALF], x_from_second[t - HALF])
        value = own[0:ALL, :]
        diff = value - near[0:ALL, :]
        edge = 0.5 * (own[ALL : ALL + 1, :] + near[ALL : ALL + 1, :])
        weighted = edge * diff
        if t >= HALF:
            weighted = weighted + own[ALL + 8 : ALL + 9, :] * value
        high, low = split(diff, 2)
        diffs[0:ALL, at] = high
        diffs[ALL : 2 * ALL, at] = low
        high, low = split(weighted, 2)
        scaled[0:ALL, at] = high
        scaled[LANES : LANES + ALL, at] = low
    faces = lax.dot_general(
        diffs[...], scaled[...], (((1,), (1,)), ((), ())), preferred_element_type=F32
    )
    crossed = fold(gram[0 : 2 * LANES, :], LANES)
    overlap = crossed[0:ALL]
    source = crossed[ALL:LANES]
    base = 2 * LANES
    moved = fold(gram[base : base + 2 * ALL, :], ALL) - fold(faces, ALL)
    base += 2 * ALL
    massed = fold(gram[base : base + 2 * ALL, :], ALL)
    source = jnp.concatenate([source, jnp.zeros((LANES - NEW, LANES), F32)], axis=0).T
    source = pltpu.roll(source[0:ALL, :], ALL, 1)
    lane = lanes_of((ALL, LANES))
    row = rows_of((ALL, LANES))
    diagonal = jnp.sum(jnp.where(lane == row, massed, 0.0), axis=1, keepdims=True)
    upper = jnp.where(row >= lane, overlap, massed)
    out[0:ALL, :] = jnp.where(lane < ALL, upper, source)
    extra = jnp.where(lane == ALL + 16, diagonal, pltpu.roll(sensed[...], ALL, 1))
    out[ALL : 2 * ALL, :] = jnp.where(lane < ALL, moved, extra)
    out[2 * ALL : PAYLOAD, :] = jnp.zeros((PAYLOAD - 2 * ALL, LANES), F32)


def small_dot(left, right):
    return lax.dot_general(
        left, right, (((1,), (0,)), ((), ())), preferred_element_type=F32, precision=HIGH
    )


def flip(block):
    rows, columns = block.shape
    if rows < LANES:
        block = jnp.concatenate([block, jnp.zeros((LANES - rows, columns), F32)], axis=0)
    if columns < LANES:
        block = jnp.concatenate([block, jnp.zeros((LANES, LANES - columns), F32)], axis=1)
    return block.T[0:columns, 0:rows]


def lower_inverse(gram):
    shape = (NEW, LANES)
    lane, row = lanes_of(shape), rows_of(shape)
    work = jnp.concatenate(
        [gram, jnp.zeros((NEW, LANES - NEW), F32)], axis=1
    ) + jnp.where(lane == row + NEW, 1.0, 0.0)
    for k in range(NEW):
        pivot = work[k : k + 1, k : k + 1]
        line = work[k : k + 1, :] / pivot
        factor = jnp.where(row[:, 0:1] > k, work[:, k : k + 1], 0.0)
        work = work - factor * line
    pivots = jnp.sum(jnp.where(lane == row, work, 0.0), axis=1, keepdims=True)
    return (work / jnp.sqrt(pivots))[:, NEW : 2 * NEW]


def basis_kernel(
    volume,
    region_ref,
    conductivity,
    damping,
    drift_speed,
    heat_capacity,
    summed,
    y_from_first,
    y_from_second,
    x_from_first,
    x_from_second,
    rows_in,
    basis_out,
    applied_out,
    stiff_block,
    stiff_row,
    capacity_block,
    sensor_block,
    source_block,
    rows,
    coef,
    field,
    applied,
    basis_raw,
    applied_raw,
    low_y,
    high_y,
    first,
    second,
    weights,
    sems,
    basis_sems,
    applied_sems,
):
    width = CHUNKS * LANES

    incoming = [
        pltpu.make_async_copy(rows_in.at[pl.ds(x, 8)], rows.at[pl.ds(x, 8)], sems.at[x // 8])
        for x in range(0, ROWS, 8)
    ]
    for copy in incoming:
        copy.start()
    shifts = common_shifts(conductivity, damping, drift_speed, heat_capacity)

    lane = lanes_of((ALL, LANES))
    row = rows_of((ALL, LANES))
    top = summed[0:ALL, :] * volume
    bottom = summed[ALL : 2 * ALL, :] * volume
    upper = jnp.where(lane < ALL, top, 0.0)
    low_part = jnp.where(lane <= row, upper, 0.0)
    high_part = jnp.where(lane > row, upper, 0.0)
    diagonal = jnp.where(lane == row, low_part, 0.0)
    overlap = (low_part - diagonal)[:, 0:ALL] + flip(low_part[:, 0:ALL])
    mass_diagonal = jnp.where(lane == row, bottom[:, ALL + 16 : ALL + 17], 0.0)
    massed = (high_part + mass_diagonal)[:, 0:ALL] + flip(high_part[:, 0:ALL])
    moved = flip(bottom[:, 0:ALL])
    source = top[:, ALL:LANES]
    sensed = summed[ALL : 2 * ALL, ALL : ALL + 16]

    old_gram = overlap[0:OLD, 0:OLD]
    first_weights = overlap[0:OLD, OLD:ALL]
    new_gram = overlap[OLD:ALL, OLD:ALL]
    second_weights = first_weights - small_dot(old_gram, first_weights)
    left_over = second_weights - small_dot(old_gram, second_weights)
    both = first_weights + second_weights
    both_t = flip(both)
    gram = new_gram - small_dot(flip(first_weights), both) - small_dot(both_t, left_over)
    inverse = lower_inverse(gram)
    mix = jnp.concatenate([-small_dot(inverse, both_t), inverse], axis=1)
    mix_t = flip(mix)
    mix_wide = jnp.concatenate([mix, jnp.zeros((NEW, LANES - ALL), F32)], axis=1)
    for k, piece in enumerate(split(mix_wide, 3)):
        for s in range(PARTS):
            weights[k * NEW : (k + 1) * NEW, s * LANES : (s + 1) * LANES] = piece

    conduct, drift, loss, capacity = cell_fields(
        region_ref, conductivity, damping, drift_speed, heat_capacity
    )
    shape = (ROWS, width)
    lane = lanes_of(shape)
    row = rows_of(shape)
    z_index = lane % NZ
    z_down, z_up = z_terms(conduct, z_index)
    low_half = lanes_of((1, LANES)) < NZ

    odd_x, odd_y = odd_lanes(ALONG_X), odd_lanes(ALONG_Y)

    def y_tile(at_low, r, at):
        one, two = y_from_first[r, at, :], y_from_second[r, at, :]
        return jnp.where(odd_y, one, two) if at_low else jnp.where(odd_y, two, one)

    def x_tile(at_low, j, at):
        one, two = x_from_first[j, at, :], x_from_second[j, at, :]
        return jnp.where(odd_x, one, two) if at_low else jnp.where(odd_x, two, one)

    def face_conduct(at_low):
        tile = jnp.concatenate(
            [y_tile(at_low, r, slice(ALL, ALL + 1)) for r in range(HALF)], axis=0
        )
        turned = pltpu.roll(tile, NZ, 1)
        pair = [tile, turned] if at_low else [turned, tile]
        return jnp.concatenate(pair, axis=0)

    blank = jnp.zeros((ROWS, width - LANES), F32)
    before = jnp.concatenate([face_conduct(True), blank], axis=1)
    after = jnp.concatenate([blank, face_conduct(False)], axis=1)
    near_y = jnp.where(lane < NZ, before, pltpu.roll(conduct, NZ, 1))
    far_y = jnp.where(lane >= width - NZ, after, pltpu.roll(conduct, width - NZ, 1))
    x_line = [
        jnp.concatenate(
            [x_tile(at_low, j, slice(ALL, ALL + 1)) for j in range(CHUNKS)], axis=1
        )
        for at_low in (True, False)
    ]
    near_x = jnp.where(row == 0, x_line[0], pltpu.roll(conduct, 1, 0))
    far_x = jnp.where(row == ROWS - 1, x_line[1], pltpu.roll(conduct, ROWS - 1, 0))
    keep_coef = coef_writer(coef)
    y_down, y_up = 0.5 * (conduct + near_y), 0.5 * (conduct + far_y)
    x_down, x_up = 0.5 * (conduct + near_x), 0.5 * (conduct + far_x)
    keep_coef(0, x_down + drift)
    keep_coef(1, x_up)
    keep_coef(2, y_down)
    keep_coef(3, y_up)
    keep_coef(4, jnp.where(z_index == 0, 0.0, z_down))
    keep_coef(5, jnp.where(z_index == NZ - 1, 0.0, z_up))
    keep_coef(6, -(z_down + z_up + y_down + y_up + x_down + x_up + drift + loss))

    zero_rows = jnp.zeros((LANES - ALL, width), BF16)
    for stack in (first, second):
        for s in range(PARTS):
            stack[s * LANES + ALL : (s + 1) * LANES, :] = zero_rows

    def fill(stack, tiles):
        for j, tile in enumerate(tiles):
            for s, piece in enumerate(split(tile, PARTS)):
                stack[s * LANES : s * LANES + ALL, pl.ds(j * LANES, LANES)] = piece

    def product(stack):
        result = jnp.dot(weights[...], stack[...], preferred_element_type=F32)
        return result[0:NEW] + (result[NEW : 2 * NEW] + result[2 * NEW : 3 * NEW])

    fields = slice(0, ALL)
    for at_low, place in ((True, 0), (False, ROWS + 1)):
        fill(first, [x_tile(at_low, j, fields) for j in range(CHUNKS)])
        field[place] = product(first)
    for target, at_low in ((low_y, True), (high_y, False)):
        for g in range(HALF // CHUNKS):
            stack = first if g % 2 == 0 else second
            fill(stack, [y_tile(at_low, g * CHUNKS + j, fields) for j in range(CHUNKS)])
            value = product(stack)
            for j in range(CHUNKS):
                tile = value[:, j * LANES : (j + 1) * LANES]
                turned = pltpu.roll(tile, NZ, 1)
                r = g * CHUNKS + j
                target[r] = tile if at_low else turned
                target[r + HALF] = turned if at_low else tile

    def load(stack, x):
        fill(stack, [rows[x, :, j * LANES : (j + 1) * LANES] for j in range(CHUNKS)])

    def outgoing(block):
        at = pl.ds(pl.multiple_of(block * 8, 8), 8)
        return [
            pltpu.make_async_copy(basis_raw.at[:, at, :], basis_out.at[:, at, :], basis_sems.at[block]),
            pltpu.make_async_copy(
                applied_raw.at[:, at, :], applied_out.at[:, at, :], applied_sems.at[block]
            ),
        ]

    def flush(block):
        start = pl.multiple_of(block * 8, 8)
        turn_back(field, basis_raw, start, 1, NEW)
        turn_back(applied, applied_raw, start, 0, NEW)
        for copy in outgoing(block):
            copy.start()

    def keep(x, stack):
        field[x + 1] = product(stack)

    def apply(x):
        mid = [field[x + 1, :, j * LANES : (j + 1) * LANES] for j in range(CHUNKS)]
        swapped = [pltpu.roll(value, NZ, 1) for value in mid]
        for j in range(CHUNKS):
            here = slice(j * LANES, (j + 1) * LANES)
            before_j = swapped[j - 1] if j > 0 else low_y[x]
            after_j = swapped[j + 1] if j < CHUNKS - 1 else high_y[x]
            left = jnp.where(low_half, before_j, swapped[j])
            right = jnp.where(low_half, swapped[j], after_j)

            def scale(index):
                return coef[index * CHUNKS + j, pl.ds(x, 1), :]

            value = mid[j]
            applied[x, :, here] = (
                scale(0) * field[x, :, here]
                + scale(1) * field[x + 2, :, here]
                + scale(2) * left
                + scale(3) * right
                + scale(4) * pltpu.roll(value, 1, 1)
                + scale(5) * pltpu.roll(value, LANES - 1, 1)
                + scale(6) * value
            )

    for copy in incoming:
        copy.wait()
    load(first, 0)
    load(second, 1)
    keep(0, first)

    def step(i, carry):
        x = 2 * i + 1
        keep(x, second)
        load(first, x + 1)
        apply(x - 1)
        keep(x + 1, first)
        load(second, x + 2)
        apply(x)
        pl.when((i + 1) % 4 == 0)(lambda: flush((i + 1) // 4 - 1))
        return carry

    lax.fori_loop(0, ROWS // 2 - 1, step, 0)
    keep(ROWS - 1, second)
    apply(ROWS - 2)
    apply(ROWS - 1)
    flush(ROWS // 8 - 1)

    outside = small_dot(left_over, flip(inverse))
    unit = jnp.where(
        lanes_of((NEW, NEW)) == rows_of((NEW, NEW)), 1.0, 0.0
    )
    columns = small_dot(moved, mix_t)
    stiff_columns = columns[0:OLD] - shifts[0] * outside
    stiff_rest = small_dot(mix, columns) - shifts[0] * unit
    stiff_block[...] = flip(jnp.concatenate([stiff_columns, stiff_rest], axis=0))
    stiff_row[...] = small_dot(mix, moved[:, 0:OLD]) - shifts[0] * flip(outside)
    columns = small_dot(massed, mix_t)
    mass_columns = columns[0:OLD] + shifts[1] * outside
    mass_rest = small_dot(mix, columns) + shifts[1] * unit
    capacity_block[...] = flip(jnp.concatenate([mass_columns, mass_rest], axis=0))
    sensor_block[...] = flip(small_dot(mix, sensed))
    source_block[...] = small_dot(mix, source)

    for block in range(ROWS // 8):
        for copy in outgoing(block):
            copy.wait()


def swap(pieces, axes):
    return lax.all_to_all(pieces, axes, 0, 0)


def spread(block, axes):
    count = lax.axis_size(axes)
    return jnp.sum(swap(block.reshape(count, -1, LANES), axes), axis=0)


def copies_of(piece, axes):
    return swap(jnp.broadcast_to(piece[None], (lax.axis_size(axes), *piece.shape)), axes)


def gathered(piece, axes):
    return copies_of(piece, axes).reshape(-1, LANES)


def all_sum(block):
    inner, outer = ("x", "y"), ("core", "z")
    piece = spread(block, inner)
    piece = jnp.sum(copies_of(piece, outer), axis=0)
    return gathered(piece, inner)


def per_device(
    old_basis,
    new_block,
    source_matrix,
    region_map,
    conductivity,
    damping,
    drift_speed,
    heat_capacity,
    sensor_cells,
):
    width_x = old_basis.shape[1]
    width_yz = old_basis.shape[2]
    count_x = lax.axis_size(ALONG_X)
    count_y = lax.axis_size(ALONG_Y)
    volume = 1.0 / (width_x * count_x * width_yz * count_y)
    whole = pl.BlockSpec(memory_space=pltpu.VMEM)
    scalar = pl.BlockSpec(memory_space=pltpu.SMEM)
    hbm = pl.BlockSpec(memory_space=pl.ANY)
    params = pltpu.CompilerParams(vmem_limit_bytes=VMEM_LIMIT)

    def shape(*sizes):
        return jax.ShapeDtypeStruct(sizes, F32)

    def column(count, j):
        return pl.BlockSpec((count, ROWS, LANES), lambda *_: (0, 0, j))

    tables = (conductivity, damping, drift_speed, heat_capacity)

    y_first, y_second, x_first, x_second, coef = pl.pallas_call(
        pack_kernel,
        grid=(1,),
        out_shape=[
            shape(HALF, FACE, LANES),
            shape(HALF, FACE, LANES),
            shape(CHUNKS, XFACE, LANES),
            shape(CHUNKS, XFACE, LANES),
            shape(8 * CHUNKS, ROWS, LANES),
        ],
        in_specs=[whole]
        + [scalar] * 4
        + [hbm] * 2
        + [column(OLD, 0), column(OLD, CHUNKS - 1), column(NEW, 0), column(NEW, CHUNKS - 1)],
        out_specs=[whole] * 5,
        scratch_shapes=[pltpu.SemaphoreType.DMA((4 * CHUNKS,))],
        compiler_params=params,
        name="pack",
    )(
        region_map,
        *tables,
        old_basis,
        new_block,
        old_basis,
        old_basis,
        new_block,
        new_block,
    )

    def traded(value, axes, start):
        lower = range(start, lax.axis_size(axes) - 1, 2)
        pairs = [(i, i + 1) for i in lower] + [(i + 1, i) for i in lower]
        return lax.ppermute(value, axes, pairs)

    y_from_first = traded(y_first, ALONG_Y, 0)
    y_from_second = traded(y_second, ALONG_Y, 1)
    x_from_first = traded(x_first, ALONG_X, 0)
    x_from_second = traded(x_second, ALONG_X, 1)

    stack_rows = 2 * LANES + 4 * ALL
    stack_width = GROUP * CHUNKS * LANES
    gram, sensed, rows = pl.pallas_call(
        gram_kernel,
        out_shape=[
            shape(stack_rows, 2 * LANES),
            shape(ALL, LANES),
            shape(ROWS, ALL, width_yz),
        ],
        in_specs=[scalar, whole] + [hbm] * 3,
        out_specs=[whole, whole, hbm],
        scratch_shapes=[
            pltpu.VMEM((stack_rows, stack_width), BF16),
            pltpu.VMEM((stack_rows, stack_width), BF16),
            pltpu.VMEM(old_basis.shape, F32),
            pltpu.VMEM(new_block.shape, F32),
            pltpu.VMEM(source_matrix.shape, F32),
            pltpu.VMEM((ROWS, ALL, width_yz), F32),
            pltpu.VMEM((ROWS, NEW, width_yz), F32),
            pltpu.SemaphoreType.DMA((3, 4)),
            pltpu.SemaphoreType.DMA((4,)),
        ],
        compiler_params=params,
        cost_estimate=pl.CostEstimate(
            flops=2 * stack_rows * 2 * LANES * width_x * width_yz,
            bytes_accessed=(ALL + NEW) * 4 * width_x * width_yz,
            transcendentals=0,
        ),
        name="gram",
    )(sensor_cells, coef, old_basis, new_block, source_matrix)
    received = (y_from_first, y_from_second, x_from_first, x_from_second)
    received, gram = lax.optimization_barrier((received, gram))

    face_width = (HALF + CHUNKS) * LANES
    partial = pl.pallas_call(
        face_kernel,
        out_shape=shape(PAYLOAD, LANES),
        in_specs=[whole] * 10,
        out_specs=whole,
        scratch_shapes=[
            pltpu.VMEM((2 * ALL, face_width), BF16),
            pltpu.VMEM((2 * LANES, face_width), BF16),
        ],
        compiler_params=params,
        name="faces",
    )(gram, sensed, y_first, y_second, x_first, x_second, *received)

    summed = all_sum(partial)

    results = pl.pallas_call(
        functools.partial(basis_kernel, volume),
        out_shape=[
            shape(*new_block.shape),
            shape(*new_block.shape),
            shape(NEW, ALL),
            shape(NEW, OLD),
            shape(NEW, ALL),
            shape(16, NEW),
            shape(NEW, NEW),
        ],
        in_specs=[whole] + [scalar] * 4 + [whole] * 5 + [hbm],
        out_specs=[hbm, hbm] + [whole] * 5,
        scratch_shapes=[
            pltpu.VMEM((ROWS, ALL, width_yz), F32),
            pltpu.VMEM((7 * CHUNKS, ROWS, LANES), F32),
            pltpu.VMEM((ROWS + 2, NEW, width_yz), F32),
            pltpu.VMEM((ROWS, NEW, width_yz), F32),
            pltpu.VMEM(new_block.shape, F32),
            pltpu.VMEM(new_block.shape, F32),
            pltpu.VMEM((ROWS, NEW, LANES), F32),
            pltpu.VMEM((ROWS, NEW, LANES), F32),
            pltpu.VMEM((PARTS * LANES, width_yz), BF16),
            pltpu.VMEM((PARTS * LANES, width_yz), BF16),
            pltpu.VMEM((3 * NEW, PARTS * LANES), BF16),
            pltpu.SemaphoreType.DMA((4,)),
            pltpu.SemaphoreType.DMA((4,)),
            pltpu.SemaphoreType.DMA((4,)),
        ],
        compiler_params=params,
        name="basis",
    )(
        region_map,
        *tables,
        summed,
        *received,
        rows,
    )
    basis, applied, stiff_block, stiff_row, capacity_block, sensor_block, source_block = results
    return (
        basis,
        applied,
        stiff_block.T,
        stiff_row,
        capacity_block.T,
        sensor_block,
        source_block,
    )


def solution(mesh):
    mesh = jax.sharding.Mesh(mesh.devices.reshape(4, 2, 8, 4), ALONG_X + ALONG_Y)
    fields = P(None, ALONG_X, ALONG_Y)
    in_specs = (fields, fields, fields, P(ALONG_X, ALONG_Y), P(), P(), P(), P(), P())
    out_specs = (fields, fields, P(), P(), P(), P(), P())
    return jax.shard_map(
        per_device, mesh=mesh, in_specs=in_specs, out_specs=out_specs, check_vma=False
    )
```

```python
import functools

import jax
import jax.numpy as jnp
from jax import lax
from jax.experimental import pallas as pl
from jax.experimental.pallas import tpu as pltpu
from jax.sharding import PartitionSpec as P

NZ = 64
LANES = 128
OLD = 64
NEW = 32
ALL = OLD + NEW
ROWS = 32
CHUNKS = 4
HALF = ROWS // 2
GROUP = 4
PARTS = 2
FACE = ALL + 8
XFACE = ALL + 16
PAYLOAD = 2 * LANES
ALONG_X = ("x", "core")
ALONG_Y = ("z", "y")
F32 = jnp.float32
BF16 = jnp.bfloat16
HIGH = lax.Precision.HIGHEST
VMEM_LIMIT = 56 * 1024 * 1024


def position(axes):
    slow, fast = axes
    return lax.axis_index(slow) * lax.axis_size(fast) + lax.axis_index(fast)


def odd_lanes(axes):
    return jnp.broadcast_to(position(axes) % 2, (1, LANES)) == 1


def split(value, count):
    pieces = []
    for _ in range(count):
        piece = value.astype(BF16)
        pieces.append(piece)
        value = value - piece.astype(F32)
    return pieces


def lanes_of(shape):
    return lax.broadcasted_iota(jnp.int32, shape, len(shape) - 1)


def rows_of(shape):
    return lax.broadcasted_iota(jnp.int32, shape, 0)


def table_mean(table):
    total = table[0]
    for r in range(1, 8):
        total = total + table[r]
    return total * 0.125


def common_shifts(conductivity, damping, drift_speed, heat_capacity):
    loss = damping[0] * heat_capacity[0]
    for r in range(1, 8):
        loss = loss + damping[r] * heat_capacity[r]
    stiff = 6.0 * table_mean(conductivity) + table_mean(drift_speed) + loss * 0.125
    return stiff, table_mean(heat_capacity)


def turn(source, target, start, shift, fields, base):
    for f in range(0, fields, 8):
        for j in range(CHUNKS):
            here = slice(j * LANES, (j + 1) * LANES)
            tile = source[f : f + 8, pl.ds(start, 8), here]
            target[pl.ds(start + shift, 8), base + f : base + f + 8, here] = jnp.transpose(
                tile, (1, 0, 2)
            )


def turn_back(source, target, start, shift, fields):
    for f in range(0, fields, 8):
        for j in range(CHUNKS):
            here = slice(j * LANES, (j + 1) * LANES)
            tile = source[pl.ds(start + shift, 8), f : f + 8, here]
            target[f : f + 8, pl.ds(start, 8), here] = jnp.transpose(tile, (1, 0, 2))


def cell_fields(region_ref, conductivity, damping, drift_speed, heat_capacity):
    region = region_ref[...]
    conduct = jnp.zeros(region.shape, F32)
    drift = jnp.zeros(region.shape, F32)
    loss = jnp.zeros(region.shape, F32)
    capacity = jnp.zeros(region.shape, F32)
    for r in range(8):
        here = region == r
        conduct = jnp.where(here, conductivity[r], conduct)
        drift = jnp.where(here, drift_speed[r], drift)
        loss = jnp.where(here, damping[r] * heat_capacity[r], loss)
        capacity = jnp.where(here, heat_capacity[r], capacity)
    return conduct, drift, loss, capacity


def z_terms(conduct, z_index):
    low_z = jnp.where(z_index == 0, 0.0, pltpu.roll(conduct, 1, 1))
    high_z = jnp.where(z_index == NZ - 1, 0.0, pltpu.roll(conduct, conduct.shape[1] - 1, 1))
    return 0.5 * (conduct + low_z), 0.5 * (conduct + high_z)


def coef_writer(coef):
    def keep_coef(index, value):
        for j in range(CHUNKS):
            coef[index * CHUNKS + j] = value[:, j * LANES : (j + 1) * LANES]

    return keep_coef


def pack_kernel(
    region_ref,
    conductivity,
    damping,
    drift_speed,
    heat_capacity,
    old,
    new,
    old_first,
    old_last,
    new_first,
    new_last,
    y_first,
    y_second,
    x_first,
    x_second,
    coef,
    sems,
):
    width = CHUNKS * LANES
    copies = []
    odd_x, odd_y = odd_lanes(ALONG_X), odd_lanes(ALONG_Y)
    parity = position(ALONG_X) % 2
    for out, row, base in (
        (x_first, (1 - parity) * (ROWS - 1), 0),
        (x_second, parity * (ROWS - 1), 2 * CHUNKS),
    ):
        for j in range(CHUNKS):
            here = pl.ds(j * LANES, LANES)
            for field, start, count, shift in ((old, 0, OLD, 0), (new, OLD, NEW, CHUNKS)):
                copies.append(
                    pltpu.make_async_copy(
                        field.at[:, row, here],
                        out.at[j, pl.ds(start, count), :],
                        sems.at[base + shift + j],
                    )
                )
    for copy in copies:
        copy.start()
    conduct, drift, loss, capacity = cell_fields(
        region_ref, conductivity, damping, drift_speed, heat_capacity
    )
    low_half = lanes_of((1, LANES)) < NZ

    def tail(rows, value):
        return jnp.broadcast_to(value, (rows, LANES))

    def turned(ref, f, x):
        return jnp.transpose(ref[f : f + 8, x : x + 8, :], (1, 0, 2))

    for first, last, start, count in (
        (old_first, old_last, 0, OLD),
        (new_first, new_last, OLD, NEW),
    ):
        for f in range(0, count, 8):
            for x in range(0, HALF, 8):
                at = (slice(x, x + 8), slice(start + f, start + f + 8), slice(None))
                near, far = turned(last, f, x), turned(last, f, x + HALF)
                top = jnp.where(low_half[None], pltpu.roll(near, NZ, 2), far)
                near, far = turned(first, f, x), turned(first, f, x + HALF)
                low = jnp.where(low_half[None], near, pltpu.roll(far, NZ, 2))
                y_first[at] = jnp.where(odd_y[None], low, top)
                y_second[at] = jnp.where(odd_y[None], top, low)
    near, far = conduct[:HALF, width - LANES :], conduct[HALF:, width - LANES :]
    top_line = jnp.where(low_half, pltpu.roll(near, NZ, 1), far)
    near, far = conduct[:HALF, :LANES], conduct[HALF:, :LANES]
    low_line = jnp.where(low_half, near, pltpu.roll(far, NZ, 1))
    first_line = jnp.where(odd_y, low_line, top_line)
    second_line = jnp.where(odd_y, top_line, low_line)
    for r in range(HALF):
        y_first[r, ALL:FACE, :] = tail(8, first_line[r : r + 1])
        y_second[r, ALL:FACE, :] = tail(8, second_line[r : r + 1])
    for j in range(CHUNKS):
        here = slice(j * LANES, (j + 1) * LANES)
        for k, value in enumerate((conduct, drift)):
            at = slice(ALL + 8 * k, ALL + 8 * k + 8)
            top, low = value[ROWS - 1 : ROWS, here], value[0:1, here]
            x_first[j, at, :] = tail(8, jnp.where(odd_x, low, top))
            x_second[j, at, :] = tail(8, jnp.where(odd_x, top, low))

    shape = (ROWS, width)
    lane = lanes_of(shape)
    row = rows_of(shape)
    z_index = lane % NZ
    z_down, z_up = z_terms(conduct, z_index)
    half = 0.5 * conduct
    from_low_y = 0.5 * (conduct + pltpu.roll(conduct, NZ, 1))
    from_high_y = 0.5 * (conduct + pltpu.roll(conduct, width - NZ, 1))
    from_low_x = 0.5 * (conduct + pltpu.roll(conduct, 1, 0))
    from_high_x = 0.5 * (conduct + pltpu.roll(conduct, ROWS - 1, 0))
    y_down = jnp.where(lane < NZ, 0.0, from_low_y)
    y_up = jnp.where(lane >= width - NZ, 0.0, from_high_y)
    x_down = jnp.where(row == 0, 0.0, from_low_x)
    x_up = jnp.where(row == ROWS - 1, 0.0, from_high_x)
    pull = jnp.where(row == 0, 0.0, drift)
    x_last = jnp.where(position(ALONG_X) == lax.axis_size(ALONG_X) - 1, 1.0, 0.0)
    y_last = jnp.where(position(ALONG_Y) == lax.axis_size(ALONG_Y) - 1, 1.0, 0.0)
    shifts = common_shifts(conductivity, damping, drift_speed, heat_capacity)
    border = jnp.where(row == ROWS - 1, half * x_last, 0.0) + jnp.where(
        lane >= width - NZ, half * y_last, 0.0
    )
    keep_coef = coef_writer(coef)
    total = z_down + z_up + y_down + y_up + x_down + x_up + pull + loss + border
    keep_coef(0, x_down + pull)
    keep_coef(1, x_up)
    keep_coef(2, y_down)
    keep_coef(3, y_up)
    keep_coef(4, jnp.where(z_index == 0, 0.0, z_down))
    keep_coef(5, jnp.where(z_index == NZ - 1, 0.0, z_up))
    keep_coef(6, shifts[0] - total)
    keep_coef(7, capacity - shifts[1])
    for copy in copies:
        copy.wait()


def gram_kernel(
    sensor_cells, coef, old, new, source, out, sensed, rows_out, first, second, old_raw, new_raw, source_raw, rows, sources, sems, out_sems
):
    width = CHUNKS * LANES
    groups = ROWS // GROUP
    low_half = lanes_of((1, LANES)) < NZ

    def incoming(block):
        at = pl.ds(pl.multiple_of(block * 8, 8), 8)
        return [
            pltpu.make_async_copy(field.at[:, at, :], raw.at[:, at, :], sems.at[k, block])
            for k, (field, raw) in enumerate(
                ((old, old_raw), (new, new_raw), (source, source_raw))
            )
        ]

    def arrange(block):
        for copy in incoming(block):
            copy.wait()
        start = pl.multiple_of(block * 8, 8)
        turn(old_raw, rows, start, 0, OLD, 0)
        turn(new_raw, rows, start, 0, NEW, OLD)
        turn(source_raw, sources, start, 0, NEW, 0)

    def fill(stack, group):
        for r in range(GROUP):
            x = group * GROUP + r
            below = jnp.maximum(x - 1, 0)
            above = jnp.minimum(x + 1, ROWS - 1)
            mid = [rows[x, :, j * LANES : (j + 1) * LANES] for j in range(CHUNKS)]
            swapped = [pltpu.roll(value, NZ, 1) for value in mid]
            for j in range(CHUNKS):
                here = slice(j * LANES, (j + 1) * LANES)
                left = jnp.where(low_half, swapped[max(j - 1, 0)], swapped[j])
                right = jnp.where(low_half, swapped[j], swapped[min(j + 1, CHUNKS - 1)])

                def scale(index):
                    return coef[index * CHUNKS + j, pl.ds(x, 1), :]

                value = mid[j]
                moved = (
                    scale(0) * rows[below, :, here]
                    + scale(1) * rows[above, :, here]
                    + scale(2) * left
                    + scale(3) * right
                    + scale(4) * pltpu.roll(value, 1, 1)
                    + scale(5) * pltpu.roll(value, LANES - 1, 1)
                    + scale(6) * value
                )
                at = pl.ds((r * CHUNKS + j) * LANES, LANES)
                high, low = split(value, 2)
                stack[0:ALL, at] = high
                stack[LANES : LANES + ALL, at] = low
                high, low = split(sources[x, :, here], 2)
                stack[ALL:LANES, at] = high
                stack[LANES + ALL : 2 * LANES, at] = low
                base = 2 * LANES
                for item in (moved, scale(7) * value):
                    high, low = split(item, 2)
                    stack[base : base + ALL, at] = high
                    stack[base + ALL : base + 2 * ALL, at] = low
                    base += 2 * ALL

    def add(stack):
        out[...] += lax.dot_general(
            stack[...],
            stack[0 : 2 * LANES, :],
            (((1,), (1,)), ((), ())),
            preferred_element_type=F32,
        )

    for block in range(ROWS // 8):
        for copy in incoming(block):
            copy.start()
    out[...] = jnp.zeros(out.shape, F32)
    arrange(0)
    fill(first, 0)

    def step(i, carry):
        arrange(i + 1)
        add(first)
        fill(second, 2 * i + 1)
        add(second)
        fill(first, 2 * i + 2)
        return carry

    lax.fori_loop(0, groups // 2 - 1, step, 0)
    outgoing = [
        pltpu.make_async_copy(rows.at[pl.ds(x, 8)], rows_out.at[pl.ds(x, 8)], out_sems.at[x // 8])
        for x in range(0, ROWS, 8)
    ]
    for copy in outgoing:
        copy.start()
    add(first)
    fill(second, groups - 1)
    add(second)

    lane = lanes_of((ALL, LANES))
    sensed[...] = jnp.zeros(sensed.shape, F32)
    row_span = width * lax.axis_size(ALONG_Y)
    index_x, index_y = position(ALONG_X), position(ALONG_Y)

    def sense(p, carry):
        cell = sensor_cells[p]
        x_global = cell // row_span
        remainder = cell % row_span
        inside = (x_global // ROWS == index_x) & (remainder // width == index_y)

        @pl.when(inside)
        def _():
            x = x_global % ROWS
            column = remainder % width
            found = jnp.zeros((ALL, LANES), F32)
            for j in range(CHUNKS):
                value = rows[x, :, j * LANES : (j + 1) * LANES]
                found = jnp.where(lane == column - j * LANES, value, found)
            picked = jnp.sum(found, axis=1, keepdims=True)
            sensed[...] = jnp.where(lane == p, picked, sensed[...])

        return carry

    lax.fori_loop(0, sensor_cells.shape[0], sense, 0)
    for copy in outgoing:
        copy.wait()


def fold(block, rows):
    return (
        block[0:rows, 0:LANES]
        + block[rows : 2 * rows, 0:LANES]
        + (block[0:rows, LANES:] + block[rows : 2 * rows, LANES:])
    )


def face_kernel(
    gram,
    sensed,
    y_first,
    y_second,
    x_first,
    x_second,
    y_from_first,
    y_from_second,
    x_from_first,
    x_from_second,
    out,
    diffs,
    scaled,
):
    odd_x, odd_y = odd_lanes(ALONG_X), odd_lanes(ALONG_Y)
    tiles = HALF + CHUNKS
    zero_rows = jnp.zeros((LANES - ALL, tiles * LANES), BF16)
    scaled[ALL:LANES, :] = zero_rows
    scaled[LANES + ALL : 2 * LANES, :] = zero_rows
    for t in range(tiles):
        at = pl.ds(t * LANES, LANES)
        if t < HALF:
            own = jnp.where(odd_y, y_first[t], y_second[t])
            near = jnp.where(odd_y, y_from_first[t], y_from_second[t])
        else:
            own = jnp.where(odd_x, x_first[t - HALF], x_second[t - HALF])
            near = jnp.where(odd_x, x_from_first[t - HALF], x_from_second[t - HALF])
        value = own[0:ALL, :]
        diff = value - near[0:ALL, :]
        edge = 0.5 * (own[ALL : ALL + 1, :] + near[ALL : ALL + 1, :])
        weighted = edge * diff
        if t >= HALF:
            weighted = weighted + own[ALL + 8 : ALL + 9, :] * value
        high, low = split(diff, 2)
        diffs[0:ALL, at] = high
        diffs[ALL : 2 * ALL, at] = low
        high, low = split(weighted, 2)
        scaled[0:ALL, at] = high
        scaled[LANES : LANES + ALL, at] = low
    faces = lax.dot_general(
        diffs[...], scaled[...], (((1,), (1,)), ((), ())), preferred_element_type=F32
    )
    crossed = fold(gram[0 : 2 * LANES, :], LANES)
    overlap = crossed[0:ALL]
    source = crossed[ALL:LANES]
    base = 2 * LANES
    moved = fold(gram[base : base + 2 * ALL, :], ALL) - fold(faces, ALL)
    base += 2 * ALL
    massed = fold(gram[base : base + 2 * ALL, :], ALL)
    source = jnp.concatenate([source, jnp.zeros((LANES - NEW, LANES), F32)], axis=0).T
    source = pltpu.roll(source[0:ALL, :], ALL, 1)
    lane = lanes_of((ALL, LANES))
    row = rows_of((ALL, LANES))
    diagonal = jnp.sum(jnp.where(lane == row, massed, 0.0), axis=1, keepdims=True)
    upper = jnp.where(row >= lane, overlap, massed)
    out[0:ALL, :] = jnp.where(lane < ALL, upper, source)
    extra = jnp.where(lane == ALL + 16, diagonal, pltpu.roll(sensed[...], ALL, 1))
    out[ALL : 2 * ALL, :] = jnp.where(lane < ALL, moved, extra)
    out[2 * ALL : PAYLOAD, :] = jnp.zeros((PAYLOAD - 2 * ALL, LANES), F32)


def small_dot(left, right):
    return lax.dot_general(
        left, right, (((1,), (0,)), ((), ())), preferred_element_type=F32, precision=HIGH
    )


def flip(block):
    rows, columns = block.shape
    if rows < LANES:
        block = jnp.concatenate([block, jnp.zeros((LANES - rows, columns), F32)], axis=0)
    if columns < LANES:
        block = jnp.concatenate([block, jnp.zeros((LANES, LANES - columns), F32)], axis=1)
    return block.T[0:columns, 0:rows]


def lower_inverse(gram):
    shape = (NEW, LANES)
    lane, row = lanes_of(shape), rows_of(shape)
    work = jnp.concatenate(
        [gram, jnp.zeros((NEW, LANES - NEW), F32)], axis=1
    ) + jnp.where(lane == row + NEW, 1.0, 0.0)
    for k in range(NEW):
        pivot = work[k : k + 1, k : k + 1]
        line = work[k : k + 1, :] / pivot
        factor = jnp.where(row[:, 0:1] > k, work[:, k : k + 1], 0.0)
        work = work - factor * line
    pivots = jnp.sum(jnp.where(lane == row, work, 0.0), axis=1, keepdims=True)
    return (work / jnp.sqrt(pivots))[:, NEW : 2 * NEW]


def basis_kernel(
    volume,
    region_ref,
    conductivity,
    damping,
    drift_speed,
    heat_capacity,
    summed,
    y_from_first,
    y_from_second,
    x_from_first,
    x_from_second,
    rows_in,
    basis_out,
    applied_out,
    stiff_block,
    stiff_row,
    capacity_block,
    sensor_block,
    source_block,
    rows,
    coef,
    field,
    applied,
    basis_raw,
    applied_raw,
    low_y,
    high_y,
    first,
    second,
    weights,
    sems,
    basis_sems,
    applied_sems,
):
    width = CHUNKS * LANES

    incoming = [
        pltpu.make_async_copy(rows_in.at[pl.ds(x, 8)], rows.at[pl.ds(x, 8)], sems.at[x // 8])
        for x in range(0, ROWS, 8)
    ]
    for copy in incoming:
        copy.start()
    shifts = common_shifts(conductivity, damping, drift_speed, heat_capacity)

    lane = lanes_of((ALL, LANES))
    row = rows_of((ALL, LANES))
    top = summed[0:ALL, :] * volume
    bottom = summed[ALL : 2 * ALL, :] * volume
    upper = jnp.where(lane < ALL, top, 0.0)
    low_part = jnp.where(lane <= row, upper, 0.0)
    high_part = jnp.where(lane > row, upper, 0.0)
    diagonal = jnp.where(lane == row, low_part, 0.0)
    overlap = (low_part - diagonal)[:, 0:ALL] + flip(low_part[:, 0:ALL])
    mass_diagonal = jnp.where(lane == row, bottom[:, ALL + 16 : ALL + 17], 0.0)
    massed = (high_part + mass_diagonal)[:, 0:ALL] + flip(high_part[:, 0:ALL])
    moved = flip(bottom[:, 0:ALL])
    source = top[:, ALL:LANES]
    sensed = summed[ALL : 2 * ALL, ALL : ALL + 16]

    old_gram = overlap[0:OLD, 0:OLD]
    first_weights = overlap[0:OLD, OLD:ALL]
    new_gram = overlap[OLD:ALL, OLD:ALL]
    second_weights = first_weights - small_dot(old_gram, first_weights)
    left_over = second_weights - small_dot(old_gram, second_weights)
    both = first_weights + second_weights
    both_t = flip(both)
    gram = new_gram - small_dot(flip(first_weights), both) - small_dot(both_t, left_over)
    inverse = lower_inverse(gram)
    mix = jnp.concatenate([-small_dot(inverse, both_t), inverse], axis=1)
    mix_t = flip(mix)
    mix_wide = jnp.concatenate([mix, jnp.zeros((NEW, LANES - ALL), F32)], axis=1)
    for k, piece in enumerate(split(mix_wide, 3)):
        for s in range(PARTS):
            weights[k * NEW : (k + 1) * NEW, s * LANES : (s + 1) * LANES] = piece

    conduct, drift, loss, capacity = cell_fields(
        region_ref, conductivity, damping, drift_speed, heat_capacity
    )
    shape = (ROWS, width)
    lane = lanes_of(shape)
    row = rows_of(shape)
    z_index = lane % NZ
    z_down, z_up = z_terms(conduct, z_index)
    low_half = lanes_of((1, LANES)) < NZ

    odd_x, odd_y = odd_lanes(ALONG_X), odd_lanes(ALONG_Y)

    def y_tile(at_low, r, at):
        one, two = y_from_first[r, at, :], y_from_second[r, at, :]
        return jnp.where(odd_y, one, two) if at_low else jnp.where(odd_y, two, one)

    def x_tile(at_low, j, at):
        one, two = x_from_first[j, at, :], x_from_second[j, at, :]
        return jnp.where(odd_x, one, two) if at_low else jnp.where(odd_x, two, one)

    def face_conduct(at_low):
        tile = jnp.concatenate(
            [y_tile(at_low, r, slice(ALL, ALL + 1)) for r in range(HALF)], axis=0
        )
        turned = pltpu.roll(tile, NZ, 1)
        pair = [tile, turned] if at_low else [turned, tile]
        return jnp.concatenate(pair, axis=0)

    blank = jnp.zeros((ROWS, width - LANES), F32)
    before = jnp.concatenate([face_conduct(True), blank], axis=1)
    after = jnp.concatenate([blank, face_conduct(False)], axis=1)
    near_y = jnp.where(lane < NZ, before, pltpu.roll(conduct, NZ, 1))
    far_y = jnp.where(lane >= width - NZ, after, pltpu.roll(conduct, width - NZ, 1))
    x_line = [
        jnp.concatenate(
            [x_tile(at_low, j, slice(ALL, ALL + 1)) for j in range(CHUNKS)], axis=1
        )
        for at_low in (True, False)
    ]
    near_x = jnp.where(row == 0, x_line[0], pltpu.roll(conduct, 1, 0))
    far_x = jnp.where(row == ROWS - 1, x_line[1], pltpu.roll(conduct, ROWS - 1, 0))
    keep_coef = coef_writer(coef)
    y_down, y_up = 0.5 * (conduct + near_y), 0.5 * (conduct + far_y)
    x_down, x_up = 0.5 * (conduct + near_x), 0.5 * (conduct + far_x)
    keep_coef(0, x_down + drift)
    keep_coef(1, x_up)
    keep_coef(2, y_down)
    keep_coef(3, y_up)
    keep_coef(4, jnp.where(z_index == 0, 0.0, z_down))
    keep_coef(5, jnp.where(z_index == NZ - 1, 0.0, z_up))
    keep_coef(6, -(z_down + z_up + y_down + y_up + x_down + x_up + drift + loss))

    zero_rows = jnp.zeros((LANES - ALL, width), BF16)
    for stack in (first, second):
        for s in range(PARTS):
            stack[s * LANES + ALL : (s + 1) * LANES, :] = zero_rows

    def fill(stack, tiles):
        for j, tile in enumerate(tiles):
            for s, piece in enumerate(split(tile, PARTS)):
                stack[s * LANES : s * LANES + ALL, pl.ds(j * LANES, LANES)] = piece

    def product(stack):
        result = jnp.dot(weights[...], stack[...], preferred_element_type=F32)
        return result[0:NEW] + (result[NEW : 2 * NEW] + result[2 * NEW : 3 * NEW])

    fields = slice(0, ALL)
    for at_low, place in ((True, 0), (False, ROWS + 1)):
        fill(first, [x_tile(at_low, j, fields) for j in range(CHUNKS)])
        field[place] = product(first)
    for target, at_low in ((low_y, True), (high_y, False)):
        for g in range(HALF // CHUNKS):
            stack = first if g % 2 == 0 else second
            fill(stack, [y_tile(at_low, g * CHUNKS + j, fields) for j in range(CHUNKS)])
            value = product(stack)
            for j in range(CHUNKS):
                tile = value[:, j * LANES : (j + 1) * LANES]
                turned = pltpu.roll(tile, NZ, 1)
                r = g * CHUNKS + j
                target[r] = tile if at_low else turned
                target[r + HALF] = turned if at_low else tile

    def load(stack, x):
        fill(stack, [rows[x, :, j * LANES : (j + 1) * LANES] for j in range(CHUNKS)])

    def outgoing(block):
        at = pl.ds(pl.multiple_of(block * 8, 8), 8)
        return [
            pltpu.make_async_copy(basis_raw.at[:, at, :], basis_out.at[:, at, :], basis_sems.at[block]),
            pltpu.make_async_copy(
                applied_raw.at[:, at, :], applied_out.at[:, at, :], applied_sems.at[block]
            ),
        ]

    def flush(block):
        start = pl.multiple_of(block * 8, 8)
        turn_back(field, basis_raw, start, 1, NEW)
        turn_back(applied, applied_raw, start, 0, NEW)
        for copy in outgoing(block):
            copy.start()

    def keep(x, stack):
        field[x + 1] = product(stack)

    def apply(x):
        mid = [field[x + 1, :, j * LANES : (j + 1) * LANES] for j in range(CHUNKS)]
        swapped = [pltpu.roll(value, NZ, 1) for value in mid]
        for j in range(CHUNKS):
            here = slice(j * LANES, (j + 1) * LANES)
            before_j = swapped[j - 1] if j > 0 else low_y[x]
            after_j = swapped[j + 1] if j < CHUNKS - 1 else high_y[x]
            left = jnp.where(low_half, before_j, swapped[j])
            right = jnp.where(low_half, swapped[j], after_j)

            def scale(index):
                return coef[index * CHUNKS + j, pl.ds(x, 1), :]

            value = mid[j]
            applied[x, :, here] = (
                scale(0) * field[x, :, here]
                + scale(1) * field[x + 2, :, here]
                + scale(2) * left
                + scale(3) * right
                + scale(4) * pltpu.roll(value, 1, 1)
                + scale(5) * pltpu.roll(value, LANES - 1, 1)
                + scale(6) * value
            )

    for copy in incoming:
        copy.wait()
    load(first, 0)
    load(second, 1)
    keep(0, first)

    def step(i, carry):
        x = 2 * i + 1
        keep(x, second)
        load(first, x + 1)
        apply(x - 1)
        keep(x + 1, first)
        load(second, x + 2)
        apply(x)
        pl.when((i + 1) % 4 == 0)(lambda: flush((i + 1) // 4 - 1))
        return carry

    lax.fori_loop(0, ROWS // 2 - 1, step, 0)
    keep(ROWS - 1, second)
    apply(ROWS - 2)
    apply(ROWS - 1)
    flush(ROWS // 8 - 1)

    outside = small_dot(left_over, flip(inverse))
    unit = jnp.where(
        lanes_of((NEW, NEW)) == rows_of((NEW, NEW)), 1.0, 0.0
    )
    columns = small_dot(moved, mix_t)
    stiff_columns = columns[0:OLD] - shifts[0] * outside
    stiff_rest = small_dot(mix, columns) - shifts[0] * unit
    stiff_block[...] = flip(jnp.concatenate([stiff_columns, stiff_rest], axis=0))
    stiff_row[...] = small_dot(mix, moved[:, 0:OLD]) - shifts[0] * flip(outside)
    columns = small_dot(massed, mix_t)
    mass_columns = columns[0:OLD] + shifts[1] * outside
    mass_rest = small_dot(mix, columns) + shifts[1] * unit
    capacity_block[...] = flip(jnp.concatenate([mass_columns, mass_rest], axis=0))
    sensor_block[...] = flip(small_dot(mix, sensed))
    source_block[...] = small_dot(mix, source)

    for block in range(ROWS // 8):
        for copy in outgoing(block):
            copy.wait()


def swap(pieces, axes):
    return lax.all_to_all(pieces, axes, 0, 0)


def spread(block, axes):
    count = lax.axis_size(axes)
    return jnp.sum(swap(block.reshape(count, -1, LANES), axes), axis=0)


def copies_of(piece, axes):
    return swap(jnp.broadcast_to(piece[None], (lax.axis_size(axes), *piece.shape)), axes)


def gathered(piece, axes):
    return copies_of(piece, axes).reshape(-1, LANES)


def all_sum(block):
    inner, outer = ("x", "y"), ("core", "z")
    piece = spread(block, inner)
    piece = jnp.sum(copies_of(piece, outer), axis=0)
    return gathered(piece, inner)


def per_device(
    old_basis,
    new_block,
    source_matrix,
    region_map,
    conductivity,
    damping,
    drift_speed,
    heat_capacity,
    sensor_cells,
):
    width_x = old_basis.shape[1]
    width_yz = old_basis.shape[2]
    count_x = lax.axis_size(ALONG_X)
    count_y = lax.axis_size(ALONG_Y)
    volume = 1.0 / (width_x * count_x * width_yz * count_y)
    whole = pl.BlockSpec(memory_space=pltpu.VMEM)
    scalar = pl.BlockSpec(memory_space=pltpu.SMEM)
    hbm = pl.BlockSpec(memory_space=pl.ANY)
    params = pltpu.CompilerParams(vmem_limit_bytes=VMEM_LIMIT)

    def shape(*sizes):
        return jax.ShapeDtypeStruct(sizes, F32)

    def column(count, j):
        return pl.BlockSpec((count, ROWS, LANES), lambda *_: (0, 0, j))

    tables = (conductivity, damping, drift_speed, heat_capacity)

    y_first, y_second, x_first, x_second, coef = pl.pallas_call(
        pack_kernel,
        grid=(1,),
        out_shape=[
            shape(HALF, FACE, LANES),
            shape(HALF, FACE, LANES),
            shape(CHUNKS, XFACE, LANES),
            shape(CHUNKS, XFACE, LANES),
            shape(8 * CHUNKS, ROWS, LANES),
        ],
        in_specs=[whole]
        + [scalar] * 4
        + [hbm] * 2
        + [column(OLD, 0), column(OLD, CHUNKS - 1), column(NEW, 0), column(NEW, CHUNKS - 1)],
        out_specs=[whole] * 5,
        scratch_shapes=[pltpu.SemaphoreType.DMA((4 * CHUNKS,))],
        compiler_params=params,
        name="pack",
    )(
        region_map,
        *tables,
        old_basis,
        new_block,
        old_basis,
        old_basis,
        new_block,
        new_block,
    )

    def traded(value, axes, start):
        lower = range(start, lax.axis_size(axes) - 1, 2)
        pairs = [(i, i + 1) for i in lower] + [(i + 1, i) for i in lower]
        return lax.ppermute(value, axes, pairs)

    y_from_first = traded(y_first, ALONG_Y, 0)
    y_from_second = traded(y_second, ALONG_Y, 1)
    x_from_first = traded(x_first, ALONG_X, 0)
    x_from_second = traded(x_second, ALONG_X, 1)

    stack_rows = 2 * LANES + 4 * ALL
    stack_width = GROUP * CHUNKS * LANES
    gram, sensed, rows = pl.pallas_call(
        gram_kernel,
        out_shape=[
            shape(stack_rows, 2 * LANES),
            shape(ALL, LANES),
            shape(ROWS, ALL, width_yz),
        ],
        in_specs=[scalar, whole] + [hbm] * 3,
        out_specs=[whole, whole, hbm],
        scratch_shapes=[
            pltpu.VMEM((stack_rows, stack_width), BF16),
            pltpu.VMEM((stack_rows, stack_width), BF16),
            pltpu.VMEM(old_basis.shape, F32),
            pltpu.VMEM(new_block.shape, F32),
            pltpu.VMEM(source_matrix.shape, F32),
            pltpu.VMEM((ROWS, ALL, width_yz), F32),
            pltpu.VMEM((ROWS, NEW, width_yz), F32),
            pltpu.SemaphoreType.DMA((3, 4)),
            pltpu.SemaphoreType.DMA((4,)),
        ],
        compiler_params=params,
        cost_estimate=pl.CostEstimate(
            flops=2 * stack_rows * 2 * LANES * width_x * width_yz,
            bytes_accessed=(ALL + NEW) * 4 * width_x * width_yz,
            transcendentals=0,
        ),
        name="gram",
    )(sensor_cells, coef, old_basis, new_block, source_matrix)
    received = (y_from_first, y_from_second, x_from_first, x_from_second)
    received, gram = lax.optimization_barrier((received, gram))

    face_width = (HALF + CHUNKS) * LANES
    partial = pl.pallas_call(
        face_kernel,
        out_shape=shape(PAYLOAD, LANES),
        in_specs=[whole] * 10,
        out_specs=whole,
        scratch_shapes=[
            pltpu.VMEM((2 * ALL, face_width), BF16),
            pltpu.VMEM((2 * LANES, face_width), BF16),
        ],
        compiler_params=params,
        name="faces",
    )(gram, sensed, y_first, y_second, x_first, x_second, *received)

    summed = all_sum(partial)

    results = pl.pallas_call(
        functools.partial(basis_kernel, volume),
        out_shape=[
            shape(*new_block.shape),
            shape(*new_block.shape),
            shape(NEW, ALL),
            shape(NEW, OLD),
            shape(NEW, ALL),
            shape(16, NEW),
            shape(NEW, NEW),
        ],
        in_specs=[whole] + [scalar] * 4 + [whole] * 5 + [hbm],
        out_specs=[hbm, hbm] + [whole] * 5,
        scratch_shapes=[
            pltpu.VMEM((ROWS, ALL, width_yz), F32),
            pltpu.VMEM((7 * CHUNKS, ROWS, LANES), F32),
            pltpu.VMEM((ROWS + 2, NEW, width_yz), F32),
            pltpu.VMEM((ROWS, NEW, width_yz), F32),
            pltpu.VMEM(new_block.shape, F32),
            pltpu.VMEM(new_block.shape, F32),
            pltpu.VMEM((ROWS, NEW, LANES), F32),
            pltpu.VMEM((ROWS, NEW, LANES), F32),
            pltpu.VMEM((PARTS * LANES, width_yz), BF16),
            pltpu.VMEM((PARTS * LANES, width_yz), BF16),
            pltpu.VMEM((3 * NEW, PARTS * LANES), BF16),
            pltpu.SemaphoreType.DMA((4,)),
            pltpu.SemaphoreType.DMA((4,)),
            pltpu.SemaphoreType.DMA((4,)),
        ],
        compiler_params=params,
        name="basis",
    )(
        region_map,
        *tables,
        summed,
        *received,
        rows,
    )
    basis, applied, stiff_block, stiff_row, capacity_block, sensor_block, source_block = results
    return (
        basis,
        applied,
        stiff_block.T,
        stiff_row,
        capacity_block.T,
        sensor_block,
        source_block,
    )


def solution(mesh):
    mesh = jax.sharding.Mesh(mesh.devices.reshape(4, 2, 8, 4), ALONG_X + ALONG_Y)
    fields = P(None, ALONG_X, ALONG_Y)
    in_specs = (fields, fields, fields, P(ALONG_X, ALONG_Y), P(), P(), P(), P(), P())
    out_specs = (fields, fields, P(), P(), P(), P(), P())
    return jax.shard_map(
        per_device, mesh=mesh, in_specs=in_specs, out_specs=out_specs, check_vma=False
    )
```
